128 devices in a mesh: prefix: 8 (over z_lo, y), resp: 8 (over x, core), mp: 2 (over z_hi).
Axes of the slice: x: 4, y: 4, z: 4 (z_hi: 2, z_lo: 2; z = z_hi * 2 + z_lo), core: 2. Of those that a mesh axis runs over, the one named last changes fastest.
Arguments:
- queries: bfloat16 [16, 1024, 32, 128], P('prefix', ('resp', 'mp')), may hold values from -6 to 6
- resp_keys: bfloat16 [16, 1024, 4, 128], P('prefix', ('resp', 'mp')), may hold values from -6 to 6
- resp_values: bfloat16 [16, 1024, 4, 128], P('prefix', ('resp', 'mp')), may hold values from -6 to 6
- prefix_keys: bfloat16 [2, 2048, 4, 128], P(None, 'prefix', 'mp'), may hold values from -6 to 6
- prefix_values: bfloat16 [2, 2048, 4, 128], P(None, 'prefix', 'mp'), may hold values from -6 to 6
- grad_out: bfloat16 [16, 1024, 32, 128], P('prefix', ('resp', 'mp')), may hold values from -6 to 6
- prompt_ids: int32 [16], replicated, may hold values from 0 to 1
- prefix_lengths: int32 [2], replicated, may hold values from 512 to 2048, as said below
- resp_lengths: int32 [16], replicated, may hold values from 1 to 1024, 10240 in all
Outputs:
- attention: bfloat16 [16, 1024, 32, 128], P('prefix', ('resp', 'mp'))
- d_queries: bfloat16 [16, 1024, 32, 128], P('prefix', ('resp', 'mp'))
- d_resp_keys: bfloat16 [16, 1024, 4, 128], P('prefix', ('resp', 'mp'))
- d_resp_values: bfloat16 [16, 1024, 4, 128], P('prefix', ('resp', 'mp'))
- d_prefix_keys: bfloat16 [2, 2048, 4, 128], P(None, 'prefix', 'mp')
- d_prefix_values: bfloat16 [2, 2048, 4, 128], P(None, 'prefix', 'mp')
The draws below stay inside these ranges and needn't reach their ends.
Inputs may be any that keep to these rules, and one draw needn't show every extreme that they name: `prefix_lengths`: some prompt has all 2048 prefix positions valid. `resp_lengths`: some response has all 1024 positions valid.
All inputs are finite; a program needn't handle non-finite values.
Results may differ from the reference program's by a relative error of at most 0.04.
Values may be sent and summed in bfloat16 or wider, within the bound.
A program may use at most 192 MiB of HBM per device.

```python
import math
import jax
import jax.numpy as jnp
import numpy as np
from jax import lax

HD = 128
QH = 32
KVH = 4
PREFIX = 2048
RLEN = 1024
PROMPTS = 2
RESPONSES = 16


def draw_queries(key, part):
    key = jax.random.fold_in(key, 11)
    first = jax.random.fold_in(key, 0)
    shape = (RESPONSES, RLEN, QH, HD)
    values = jax.random.truncated_normal(first, -6.0, 6.0, shape, jnp.float32)
    return values.astype(jnp.bfloat16)


def draw_prefix_keys(key, part):
    key = jax.random.fold_in(key, 13)
    shape = (PROMPTS, PREFIX, KVH, HD)
    values = jax.random.truncated_normal(key, -6.0, 6.0, shape, jnp.float32)
    return values.astype(jnp.bfloat16)


def draw_prefix_lengths(key, part):
    key = jax.random.fold_in(key, 23)
    first, second = jax.random.split(key)
    lengths = jax.random.randint(first, (PROMPTS,), PREFIX // 4, PREFIX + 1, jnp.int32)
    longest = jax.random.randint(second, (), 0, PROMPTS, jnp.int32)
    return jnp.where(jnp.arange(PROMPTS, dtype=jnp.int32) == longest, PREFIX, lengths).astype(jnp.int32)


def with_ends(values, rng, least, top_value):
    longest = values.shape.index(max(values.shape))
    spots = []
    for shift in (0, 1):
        where = [jax.random.randint(jax.random.fold_in(rng, axis), (), 0, length) for axis, length in enumerate(values.shape)]
        where[longest] = (where[longest] + shift) % values.shape[longest]
        spots.append(tuple(where))
    return values.at[spots[0]].set(least).at[spots[1]].set(top_value)


def shard_levels(own_key, dims, shards, low, top_value):
    level, own = 1.0, jax.random.fold_in(own_key, 6)
    for dim, parts in shards:
        heights = jnp.exp(jax.random.uniform(jax.random.fold_in(own, dim), (parts,), jnp.float32, low / len(shards), top_value / len(shards)))
        level = level * jnp.repeat(heights, dims[dim] // parts).reshape([-1 if axis == dim else 1 for axis in range(len(dims))])
    return level


def split_up(amount, total, reach, skew):
    weights = [(1 << 20) // math.isqrt(grade ** skew) + 1 for grade in range(2, amount + 1)]
    rest, counts = total - reach - (amount - 1), [1] * (amount - 1)
    while rest > 0:
        candidates = [i for i in range(amount - 1) if counts[i] < reach]
        mass, left = sum([weights[i] for i in candidates]), rest
        for i in candidates:
            extra = min(reach - counts[i], max(1, left * weights[i] // mass), rest)
            counts[i] = counts[i] + extra
            rest = rest - extra
    return np.array([reach] + counts)


def ragged(key, amount, total, bound, slope):
    if amount == 2:
        one = jax.random.randint(key, (), max(1, total - bound), min(bound, total - 1) + 1)
        return jnp.stack([one, total - one])
    tallies = jnp.asarray(split_up(amount, total, bound, slope), jnp.int32)
    couples = (amount - 1) // 2
    giver, sink = tallies[1:1 + 2 * couples:2], tallies[2:2 + 2 * couples:2]
    slack = jnp.minimum(giver - 1, bound - sink)
    moved = jax.random.randint(jax.random.fold_in(key, 1), (couples,), 0, 1 << 20) % (slack + 1)
    tallies = tallies.at[1:1 + 2 * couples:2].set(giver - moved).at[2:2 + 2 * couples:2].set(sink + moved)
    return tallies[jax.random.permutation(jax.random.fold_in(key, 2), amount)]


def scatter_about(stream_key, shape, spread, most, shards=(), kind=jnp.bfloat16):
    level = shard_levels(stream_key, shape, shards, -0.22, 0.18) if shards else 1.0
    values = jax.random.normal(stream_key, shape, jnp.float32) * spread * level
    return jnp.minimum(jnp.maximum(values, -most), most).astype(kind)


def setup_inputs(seed: int = 0) -> dict:
    keys = jax.random.split(jax.random.key(seed), 10)
    return {
        "queries": draw_queries(jax.random.fold_in(keys[9], 71), 0),
        "resp_keys": scatter_about(keys[1], (RESPONSES, RLEN, KVH, HD), 1.0, 6.0, ((0, 8), (1, 16))),
        "resp_values": scatter_about(keys[2], (RESPONSES, RLEN, KVH, HD), 1.0, 6.0, ((0, 8), (1, 16))),
        "prefix_keys": draw_prefix_keys(jax.random.fold_in(keys[9], 71), 0),
        "prefix_values": scatter_about(keys[4], (PROMPTS, PREFIX, KVH, HD), 1.0, 6.0, ((1, 8), (2, 2))),
        "grad_out": scatter_about(keys[5], (RESPONSES, RLEN, QH, HD), 1.0, 6.0, ((0, 8), (1, 16))),
        "prompt_ids": with_ends(jax.random.randint(keys[6], (RESPONSES,), 0, PROMPTS), jax.random.fold_in(keys[6], 1), 0, PROMPTS - 1).astype(jnp.int32),
        "prefix_lengths": draw_prefix_lengths(jax.random.fold_in(keys[9], 71), 0),
        "resp_lengths": ragged(keys[8], RESPONSES, RESPONSES * RLEN * 5 // 8, RLEN, 2).astype(jnp.int32),
    }


NEG = -1e+30

def one_head(query_rows, cot_rows, key_rows, value_rows, is_valid):
    inv_root = 1.0 / math.sqrt(query_rows.shape[-1])
    scores = jnp.einsum('tgd,sd->tgs', query_rows.astype(jnp.float32), key_rows.astype(jnp.float32)) * inv_root
    scores = jnp.where(is_valid[:, None, :], scores, NEG)
    row_max = lax.optimization_barrier(jnp.max(scores, axis=-1))
    log_total = row_max + jnp.log(lax.optimization_barrier(jnp.sum(jnp.exp(scores - row_max[..., None]), axis=-1)))
    probs = jnp.exp(scores - log_total[..., None])
    weights = lax.optimization_barrier(probs.astype(jnp.bfloat16))
    attended = jnp.einsum('tgs,sd->tgd', weights.astype(jnp.float32), value_rows.astype(jnp.float32))
    attended = lax.optimization_barrier(attended.astype(jnp.bfloat16))
    row_delta = lax.optimization_barrier(jnp.sum(cot_rows.astype(jnp.float32) * attended.astype(jnp.float32), axis=-1))
    dprobs = jnp.einsum('tgd,sd->tgs', cot_rows.astype(jnp.float32), value_rows.astype(jnp.float32))
    dscores = lax.optimization_barrier((probs * (dprobs - row_delta[..., None])).astype(jnp.bfloat16))
    grad_query = (inv_root * jnp.einsum('tgs,sd->tgd', dscores.astype(jnp.float32), key_rows.astype(jnp.float32))).astype(jnp.bfloat16)
    grad_key = inv_root * jnp.einsum('tgs,tgd->sd', dscores.astype(jnp.float32), query_rows.astype(jnp.float32))
    grad_value = jnp.einsum('tgs,tgd->sd', weights.astype(jnp.float32), cot_rows.astype(jnp.float32))
    return (attended, grad_query, grad_key, grad_value)

def reference(queries, resp_keys, resp_values, prefix_keys, prefix_values, grad_out, prompt_ids, prefix_lengths, resp_lengths):
    group_size = QH // KVH
    positions = jnp.arange(RLEN, dtype=jnp.int32)
    key_index = jnp.arange(PREFIX + RLEN, dtype=jnp.int32)[None, :]
    resp_pos = key_index - PREFIX

    def per_response(response_items):
        query_rows, keys_r, values_r, cotangent, prompt, length = response_items
        keys_p = lax.dynamic_index_in_dim(prefix_keys, prompt, 0, keepdims=False)
        values_p = lax.dynamic_index_in_dim(prefix_values, prompt, 0, keepdims=False)
        prefix_len = lax.dynamic_index_in_dim(prefix_lengths, prompt, 0, keepdims=False)
        keys_all = jnp.concatenate([keys_p, keys_r], axis=0)
        values_all = jnp.concatenate([values_p, values_r], axis=0)
        is_valid = jnp.where(key_index < PREFIX, key_index < prefix_len, (resp_pos <= positions[:, None]) & (resp_pos < length))
        live_rows = positions < length
        cotangent = jnp.where(live_rows[:, None, None], cotangent, jnp.zeros_like(cotangent))
        grouped_q = query_rows.reshape(RLEN, KVH, group_size, HD).transpose(1, 0, 2, 3)
        grouped_c = cotangent.reshape(RLEN, KVH, group_size, HD).transpose(1, 0, 2, 3)

        def per_head(head_items):
            return one_head(head_items[0], head_items[1], head_items[2], head_items[3], is_valid)
        attended, grad_query, grad_key, grad_value = lax.map(per_head, (grouped_q, grouped_c, keys_all.transpose(1, 0, 2), values_all.transpose(1, 0, 2)))
        attended = attended.transpose(1, 0, 2, 3).reshape(RLEN, QH, HD)
        grad_query = grad_query.transpose(1, 0, 2, 3).reshape(RLEN, QH, HD)
        grad_key = grad_key.transpose(1, 0, 2)
        grad_value = grad_value.transpose(1, 0, 2)
        return (attended, grad_query, grad_key[:PREFIX], grad_value[:PREFIX], grad_key[PREFIX:].astype(jnp.bfloat16), grad_value[PREFIX:].astype(jnp.bfloat16))
    results = lax.map(per_response, (queries, resp_keys, resp_values, grad_out, prompt_ids, resp_lengths))
    d_prefix_keys = jax.ops.segment_sum(results[2], prompt_ids, num_segments=PROMPTS).astype(jnp.bfloat16)
    d_prefix_values = jax.ops.segment_sum(results[3], prompt_ids, num_segments=PROMPTS).astype(jnp.bfloat16)
    return (results[0], results[1], results[4], results[5], d_prefix_keys, d_prefix_values)
```

```python
import math
import jax, jax.numpy as jnp
from jax import lax
from jax.sharding import PartitionSpec as P
from jax.experimental import pallas as pl
from jax.experimental.pallas import tpu as pltpu

HD=128; PRE=2048; RL=1024; T=128; G=8; R=T*G
ROWS=2*PRE+2*RL
NT=(((1,),(1,)),((),()))
NN=(((1,),(0,)),((),()))
TN=(((0,),(0,)),((),()))
def dot(a,b,dn): return lax.dot_general(a,b,dn,preferred_element_type=jnp.float32)

def attend(KB=256, RC=256, variant="wt"):
    C2=math.log2(math.e)/math.sqrt(HD); INV=1/math.sqrt(HD)
    def kernel(meta, q_ref, c_ref, k_ref, v_ref, o_ref, dq_ref, dk_ref, dv_ref,
               qhl, qr, dr, S, Pm, mx, ls, oacc, dqacc, dkacc, dvacc, ocat, dqcat):
        pos0=meta[0]
        dkacc[...]=jnp.zeros_like(dkacc); dvacc[...]=jnp.zeros_like(dvacc)
        def prep(b, _):
            for tc in range(0,T,32):
                qf=q_ref[b,pl.ds(tc,32)].astype(jnp.float32)
                for h in range(2):
                    x=qf[:,h*G:(h+1)*G].reshape(32*G,HD)
                    rows=pl.ds(tc*G,32*G)
                    qr[h,b,rows]=x.astype(jnp.bfloat16)
                    xs=x*C2
                    hi=xs.astype(jnp.bfloat16)
                    lo=(xs-hi.astype(jnp.float32)).astype(jnp.bfloat16)
                    qhl[h,b,rows,0:HD]=hi
                    qhl[h,b,rows,HD:]=lo
            return 0
        lax.fori_loop(0,2,prep,0)
        def group(g,_):
            h=g//2; b=g%2
            prompt=meta[1+b]; length=meta[3+b]; plen=meta[5+b]
            npre=(plen+KB-1)//KB
            rk=jnp.minimum(pos0+T,length)
            nres=(rk+KB-1)//KB
            nblk=npre+nres
            def place(i):
                isp=i<npre
                j=i-npre
                row=jnp.where(isp, prompt*PRE+i*KB, 2*PRE+b*RL+j*KB)
                return isp, j, pl.multiple_of(row,KB)
            mx[...]=jnp.full_like(mx,-jnp.inf)
            ls[...]=jnp.zeros_like(ls)
            oacc[...]=jnp.zeros_like(oacc)
            def passA(i,_):
                isp,j,row=place(i)
                kb=k_ref[h,pl.ds(row,KB)]
                kk=jnp.concatenate([kb,kb],axis=1)
                col=lax.broadcasted_iota(jnp.int32,(RC,KB),1)
                base=jnp.where(isp,i*KB,j*KB)
                for rc in range(0,R,RC):
                    s=dot(qhl[h,b,pl.ds(rc,RC)],kk,NT)
                    t=pos0+rc//G+lax.broadcasted_iota(jnp.int32,(RC,1),0)//G
                    lim=jnp.where(isp,plen-1,jnp.minimum(t,length-1))-base
                    s=jnp.where(col<=lim,s,-1e30)
                    S[pl.ds(rc,RC),pl.ds(pl.multiple_of(i*KB,KB),KB)]=s
                    m=mx[pl.ds(rc,RC)]
                    for c in range(0,KB,128): m=jnp.maximum(m,s[:,c:c+128])
                    mx[pl.ds(rc,RC)]=m
                return 0
            lax.fori_loop(0,nblk,passA,0)
            for rc in range(0,R,RC):
                m=jnp.max(mx[pl.ds(rc,RC)],axis=1,keepdims=True)
                mx[pl.ds(rc,RC)]=jnp.broadcast_to(m,(RC,128))
            def passB(i,_):
                isp,j,row=place(i)
                vb=v_ref[h,pl.ds(row,KB)]
                for rc in range(0,R,RC):
                    m=mx[pl.ds(rc,RC)]
                    s=S[pl.ds(rc,RC),pl.ds(pl.multiple_of(i*KB,KB),KB)]
                    ps=[]
                    l=ls[pl.ds(rc,RC)]
                    for c in range(0,KB,128):
                        p=jnp.exp2(s[:,c:c+128]-m)
                        l=l+p
                        ps.append(p.astype(jnp.bfloat16))
                    ls[pl.ds(rc,RC)]=l
                    pb=jnp.concatenate(ps,axis=1)
                    Pm[pl.ds(rc,RC),pl.ds(pl.multiple_of(i*KB,KB),KB)]=pb
                    oacc[pl.ds(rc,RC)]+=dot(pb,vb,NN)
                return 0
            lax.fori_loop(0,nblk,passB,0)
            for rc in range(0,R,RC):
                rows=pl.ds(rc,RC)
                tr=pl.ds(rc//G,RC//G)
                l=jnp.sum(ls[rows],axis=1,keepdims=True)
                il=1.0/l
                o=(oacc[rows]*il).astype(jnp.bfloat16).astype(jnp.float32)
                ocat[h,b,rows]=o
                d=c_ref[b,tr].astype(jnp.float32)
                d=jnp.where(h==0,d[:,:G],d[:,G:]).reshape(RC,HD)
                t=pos0+rc//G+lax.broadcasted_iota(jnp.int32,(RC,1),0)//G
                d=jnp.where(t<length,d,0.0)
                delta=jnp.sum(d*o,axis=1,keepdims=True)
                dr[rows]=(d*il).astype(jnp.bfloat16)
                mx[rows]=jnp.broadcast_to(delta*il,(RC,128))
            dqacc[...]=jnp.zeros_like(dqacc)
            def passC(i,_):
                isp,j,row=place(i)
                vb=v_ref[h,pl.ds(row,KB)]
                kb=k_ref[h,pl.ds(row,KB)]
                dss=[]
                cs=pl.ds(pl.multiple_of(i*KB,KB),KB)
                for rc in range(0,R,RC):
                    rows=pl.ds(rc,RC)
                    dp=dot(dr[rows],vb,NT)
                    p=Pm[rows,cs].astype(jnp.float32)
                    dl=mx[rows]
                    ds=jnp.concatenate([p[:,c:c+128]*(dp[:,c:c+128]-dl) for c in range(0,KB,128)],axis=1).astype(jnp.bfloat16)
                    dqacc[rows]+=dot(ds,kb,NN)
                    dss.append(ds)
                ds=jnp.concatenate(dss,axis=0)
                if variant=="tn":
                    dkacc[h,pl.ds(row,KB)]+=dot(ds,qr[h,b],TN)
                    dvacc[h,pl.ds(row,KB)]+=dot(Pm[:,cs],dr[...],TN)
                else:
                    dkacc[h,pl.ds(row,KB)]+=dot(qr[h,b],ds,TN).T
                    dvacc[h,pl.ds(row,KB)]+=dot(dr[...],Pm[:,cs],TN).T
                return 0
            lax.fori_loop(0,jnp.where(length>pos0,nblk,0),passC,0)
            for rc in range(0,R,RC):
                dqcat[h,b,pl.ds(rc,RC)]=dqacc[pl.ds(rc,RC)]*INV
            return 0
        lax.fori_loop(0,4,group,0)
        def fin(b,_):
            for tc in range(0,T,32):
                rows=pl.ds(tc*G,32*G)
                for src,dst in ((ocat,o_ref),(dqcat,dq_ref)):
                    a=jnp.concatenate([src[h,b,rows].reshape(32,G,HD) for h in range(2)],axis=1)
                    dst[b,pl.ds(tc,32)]=a.astype(jnp.bfloat16)
            return 0
        lax.fori_loop(0,2,fin,0)
        def finkv(i,_):
            for h in range(2):
                rows=pl.ds(pl.multiple_of(i*512,512),512)
                dk_ref[h,rows]=(dkacc[h,rows]*INV).astype(jnp.bfloat16)
                dv_ref[h,rows]=dvacc[h,rows].astype(jnp.bfloat16)
            return 0
        lax.fori_loop(0,ROWS//512,finkv,0)
    bf=jnp.bfloat16; f32=jnp.float32
    V=pl.BlockSpec(memory_space=pltpu.VMEM)
    scratch=[pltpu.VMEM((2,2,R,2*HD),bf),pltpu.VMEM((2,2,R,HD),bf),pltpu.VMEM((R,HD),bf),
             pltpu.VMEM((R,3072),f32),pltpu.VMEM((R,3072),bf),pltpu.VMEM((R,128),f32),pltpu.VMEM((R,128),f32),
             pltpu.VMEM((R,HD),f32),pltpu.VMEM((R,HD),f32),pltpu.VMEM((2,ROWS,HD),f32),pltpu.VMEM((2,ROWS,HD),f32),
             pltpu.VMEM((2,2,R,HD),f32),pltpu.VMEM((2,2,R,HD),f32)]
    return pl.pallas_call(kernel,
        out_shape=[jax.ShapeDtypeStruct((2,T,16,HD),bf),jax.ShapeDtypeStruct((2,T,16,HD),bf),
                   jax.ShapeDtypeStruct((2,ROWS,HD),bf),jax.ShapeDtypeStruct((2,ROWS,HD),bf)],
        in_specs=[pl.BlockSpec(memory_space=pltpu.SMEM),V,V,V,V],out_specs=[V]*4,
        scratch_shapes=scratch,
        compiler_params=pltpu.CompilerParams(vmem_limit_bytes=60*2**20))


def per_device(queries, resp_keys, resp_values, prefix_keys, prefix_values, grad_out, prompt_ids, prefix_lengths, resp_lengths):
    q = lax.all_to_all(queries, "mp", split_axis=2, concat_axis=1, tiled=True)
    c = lax.all_to_all(grad_out, "mp", split_axis=2, concat_axis=1, tiled=True)
    kv = jnp.stack([resp_keys, resp_values])
    kv = lax.all_to_all(kv, "mp", split_axis=3, concat_axis=2, tiled=True)
    kv = lax.all_gather(kv.transpose(0, 3, 1, 2, 4), "resp", axis=3, tiled=True)
    pre = jnp.stack([prefix_keys, prefix_values]).transpose(0, 3, 1, 2, 4)
    pre = lax.all_gather(pre, "prefix", axis=3, tiled=True)
    flat = jnp.concatenate([pre.reshape(2, 2, 2 * PRE, HD), kv.reshape(2, 2, 2 * RL, HD)], axis=2)
    first = lax.axis_index("prefix") * 2
    prompts = lax.dynamic_slice_in_dim(prompt_ids, first, 2)
    lengths = lax.dynamic_slice_in_dim(resp_lengths, first, 2)
    pos0 = lax.axis_index("resp") * T
    meta = jnp.concatenate([pos0[None], prompts, lengths, prefix_lengths[prompts], jnp.zeros((1,), jnp.int32)]).astype(jnp.int32)
    o, dq, dk, dv = attend()(meta, q, c, flat[0], flat[1])
    terms = jnp.stack([dk, dv])
    rt = terms[:, :, 2 * PRE :].reshape(2, 2, 2, 8, T, HD)
    rt = lax.all_to_all(rt, "resp", split_axis=3, concat_axis=3, tiled=True)
    rt = jnp.sum(rt.astype(jnp.float32), axis=3).astype(jnp.bfloat16)
    rt = rt.transpose(0, 2, 3, 1, 4)
    rt = lax.all_to_all(rt, "mp", split_axis=2, concat_axis=3, tiled=True)
    pt = terms[:, :, : 2 * PRE].reshape(2, 2, 2, 64, 32, HD)
    pt = lax.all_to_all(pt, ("prefix", "resp"), split_axis=3, concat_axis=3, tiled=True)
    pt = jnp.sum(pt.astype(jnp.float32), axis=3).astype(jnp.bfloat16)
    pt = lax.all_gather(pt, "resp", axis=3, tiled=True).transpose(0, 2, 3, 1, 4)
    attention = lax.all_to_all(o, "mp", split_axis=1, concat_axis=2, tiled=True)
    d_queries = lax.all_to_all(dq, "mp", split_axis=1, concat_axis=2, tiled=True)
    return (attention, d_queries, rt[0], rt[1], pt[0], pt[1])


def solution(mesh):
    rows = P("prefix", ("resp", "mp"), None, None)
    pre = P(None, "prefix", "mp", None)
    return jax.shard_map(
        per_device,
        mesh=mesh,
        in_specs=(rows, rows, rows, pre, pre, rows, P(), P(), P()),
        out_specs=(rows, rows, rows, rows, pre, pre),
        check_vma=False,
    )
```

```python
import math
import jax, jax.numpy as jnp
from jax import lax
from jax.sharding import PartitionSpec as P
from jax.experimental import pallas as pl
from jax.experimental.pallas import tpu as pltpu

HD=128; PRE=2048; RL=1024; T=128; G=8; R=T*G
ROWS=2*PRE+2*RL
NT=(((1,),(1,)),((),()))
NN=(((1,),(0,)),((),()))
TN=(((0,),(0,)),((),()))
def dot(a,b,dn): return lax.dot_general(a,b,dn,preferred_element_type=jnp.float32)

def attend(KB=256, RC=256, variant="wt"):
    C2=math.log2(math.e)/math.sqrt(HD); INV=1/math.sqrt(HD)
    def kernel(meta, q_ref, c_ref, kv_ref, o_ref, dq_ref, dkv_ref,
               qhl, qr, dr, S, Pm, mx, ls, oacc, dqacc, dkacc, dvacc, ocat, dqcat):
        pos0=meta[0]
        dkacc[...]=jnp.zeros_like(dkacc); dvacc[...]=jnp.zeros_like(dvacc)
        def prep(b, _):
            for tc in range(0,T,32):
                qf=q_ref[b,pl.ds(tc,32)].astype(jnp.float32)
                for h in range(2):
                    x=qf[:,h*G:(h+1)*G].reshape(32*G,HD)
                    rows=pl.ds(tc*G,32*G)
                    qr[h,b,rows]=x.astype(jnp.bfloat16)
                    xs=x*C2
                    hi=xs.astype(jnp.bfloat16)
                    lo=(xs-hi.astype(jnp.float32)).astype(jnp.bfloat16)
                    qhl[h,b,rows,0:HD]=hi
                    qhl[h,b,rows,HD:]=lo
            return 0
        lax.fori_loop(0,2,prep,0)
        def group(g,_):
            h=g//2; b=g%2
            prompt=meta[1+b]; length=meta[3+b]; plen=meta[5+b]
            npre=(plen+KB-1)//KB
            rk=jnp.minimum(pos0+T,length)
            nres=(rk+KB-1)//KB
            nblk=npre+nres
            def place(i):
                isp=i<npre
                j=i-npre
                row=jnp.where(isp, prompt*PRE+i*KB, 2*PRE+b*RL+j*KB)
                return isp, j, pl.multiple_of(row,KB)
            mx[...]=jnp.full_like(mx,-jnp.inf)
            ls[...]=jnp.zeros_like(ls)
            oacc[...]=jnp.zeros_like(oacc)
            def passA(i,_):
                isp,j,row=place(i)
                kb=kv_ref[0,h,pl.ds(row,KB)]
                kk=jnp.concatenate([kb,kb],axis=1)
                col=lax.broadcasted_iota(jnp.int32,(RC,KB),1)
                base=jnp.where(isp,i*KB,j*KB)
                for rc in range(0,R,RC):
                    s=dot(qhl[h,b,pl.ds(rc,RC)],kk,NT)
                    t=pos0+rc//G+lax.broadcasted_iota(jnp.int32,(RC,1),0)//G
                    lim=jnp.where(isp,plen-1,jnp.minimum(t,length-1))-base
                    s=jnp.where(col<=lim,s,-1e30)
                    S[pl.ds(rc,RC),pl.ds(pl.multiple_of(i*KB,KB),KB)]=s
                    m=mx[pl.ds(rc,RC)]
                    for c in range(0,KB,128): m=jnp.maximum(m,s[:,c:c+128])
                    mx[pl.ds(rc,RC)]=m
                return 0
            lax.fori_loop(0,nblk,passA,0)
            for rc in range(0,R,RC):
                m=jnp.max(mx[pl.ds(rc,RC)],axis=1,keepdims=True)
                mx[pl.ds(rc,RC)]=jnp.broadcast_to(m,(RC,128))
            def passB(i,_):
                isp,j,row=place(i)
                vb=kv_ref[1,h,pl.ds(row,KB)]
                for rc in range(0,R,RC):
                    m=mx[pl.ds(rc,RC)]
                    s=S[pl.ds(rc,RC),pl.ds(pl.multiple_of(i*KB,KB),KB)]
                    ps=[]
                    l=ls[pl.ds(rc,RC)]
                    for c in range(0,KB,128):
                        p=jnp.exp2(s[:,c:c+128]-m)
                        l=l+p
                        ps.append(p.astype(jnp.bfloat16))
                    ls[pl.ds(rc,RC)]=l
                    pb=jnp.concatenate(ps,axis=1)
                    Pm[pl.ds(rc,RC),pl.ds(pl.multiple_of(i*KB,KB),KB)]=pb
                    oacc[pl.ds(rc,RC)]+=dot(pb,vb,NN)
                return 0
            lax.fori_loop(0,nblk,passB,0)
            for rc in range(0,R,RC):
                rows=pl.ds(rc,RC)
                tr=pl.ds(rc//G,RC//G)
                l=jnp.sum(ls[rows],axis=1,keepdims=True)
                il=1.0/l
                o=(oacc[rows]*il).astype(jnp.bfloat16).astype(jnp.float32)
                ocat[h,b,rows]=o
                d=c_ref[b,tr].astype(jnp.float32)
                d=jnp.where(h==0,d[:,:G],d[:,G:]).reshape(RC,HD)
                t=pos0+rc//G+lax.broadcasted_iota(jnp.int32,(RC,1),0)//G
                d=jnp.where(t<length,d,0.0)
                delta=jnp.sum(d*o,axis=1,keepdims=True)
                dr[rows]=(d*il).astype(jnp.bfloat16)
                mx[rows]=jnp.broadcast_to(delta*il,(RC,128))
            dqacc[...]=jnp.zeros_like(dqacc)
            def passC(i,_):
                isp,j,row=place(i)
                vb=kv_ref[1,h,pl.ds(row,KB)]
                kb=kv_ref[0,h,pl.ds(row,KB)]
                dss=[]
                cs=pl.ds(pl.multiple_of(i*KB,KB),KB)
                for rc in range(0,R,RC):
                    rows=pl.ds(rc,RC)
                    dp=dot(dr[rows],vb,NT)
                    p=Pm[rows,cs].astype(jnp.float32)
                    dl=mx[rows]
                    ds=jnp.concatenate([p[:,c:c+128]*(dp[:,c:c+128]-dl) for c in range(0,KB,128)],axis=1).astype(jnp.bfloat16)
                    dqacc[rows]+=dot(ds,kb,NN)
                    dss.append(ds)
                ds=jnp.concatenate(dss,axis=0)
                if variant=="tn":
                    dkacc[h,pl.ds(row,KB)]+=dot(ds,qr[h,b],TN)
                    dvacc[h,pl.ds(row,KB)]+=dot(Pm[:,cs],dr[...],TN)
                else:
                    dkacc[h,pl.ds(row,KB)]+=dot(qr[h,b],ds,TN).T
                    dvacc[h,pl.ds(row,KB)]+=dot(dr[...],Pm[:,cs],TN).T
                return 0
            lax.fori_loop(0,jnp.where(length>pos0,nblk,0),passC,0)
            for rc in range(0,R,RC):
                dqcat[h,b,pl.ds(rc,RC)]=dqacc[pl.ds(rc,RC)]*INV
            return 0
        lax.fori_loop(0,4,group,0)
        def fin(b,_):
            for tc in range(0,T,32):
                rows=pl.ds(tc*G,32*G)
                for src,dst in ((ocat,o_ref),(dqcat,dq_ref)):
                    a=jnp.concatenate([src[h,b,rows].reshape(32,G,HD) for h in range(2)],axis=1)
                    dst[b,pl.ds(tc,32)]=a.astype(jnp.bfloat16)
            return 0
        lax.fori_loop(0,2,fin,0)
        def finkv(i,_):
            for h in range(2):
                rows=pl.ds(pl.multiple_of(i*512,512),512)
                dkv_ref[0,h,rows]=(dkacc[h,rows]*INV).astype(jnp.bfloat16)
                dkv_ref[1,h,rows]=dvacc[h,rows].astype(jnp.bfloat16)
            return 0
        lax.fori_loop(0,ROWS//512,finkv,0)
    bf=jnp.bfloat16; f32=jnp.float32
    V=pl.BlockSpec(memory_space=pltpu.VMEM)
    scratch=[pltpu.VMEM((2,2,R,2*HD),bf),pltpu.VMEM((2,2,R,HD),bf),pltpu.VMEM((R,HD),bf),
             pltpu.VMEM((R,3072),f32),pltpu.VMEM((R,3072),bf),pltpu.VMEM((R,128),f32),pltpu.VMEM((R,128),f32),
             pltpu.VMEM((R,HD),f32),pltpu.VMEM((R,HD),f32),pltpu.VMEM((2,ROWS,HD),f32),pltpu.VMEM((2,ROWS,HD),f32),
             pltpu.VMEM((2,2,R,HD),f32),pltpu.VMEM((2,2,R,HD),f32)]
    return pl.pallas_call(kernel,
        out_shape=[jax.ShapeDtypeStruct((2,T,16,HD),bf),jax.ShapeDtypeStruct((2,T,16,HD),bf),
                   jax.ShapeDtypeStruct((2,2,ROWS,HD),bf)],
        in_specs=[pl.BlockSpec(memory_space=pltpu.SMEM),V,V,V],out_specs=[V]*3,
        scratch_shapes=scratch,
        compiler_params=pltpu.CompilerParams(vmem_limit_bytes=60*2**20))


MESH = pl.DeviceIdType.MESH
HBM = pl.BlockSpec(memory_space=pl.ANY)
VM = pl.BlockSpec(memory_space=pltpu.VMEM)
BF = jnp.bfloat16
F32 = jnp.float32


class Mover:
    def __init__(self, send, recv, local):
        self.send, self.recv, self.local, self.n, self.m = send, recv, local, 0, 0
        self.remote, self.near = [], []

    def to(self, src, dst, where):
        cp = pltpu.make_async_remote_copy(
            src_ref=src, dst_ref=dst, send_sem=self.send.at[self.n], recv_sem=self.recv.at[self.n],
            device_id=where, device_id_type=MESH)
        self.n += 1
        cp.start()
        self.remote.append(cp)
        return cp

    def here(self, src, dst):
        cp = pltpu.make_async_copy(src, dst, self.local.at[self.m])
        self.m += 1
        cp.start()
        return cp

    def drain(self):
        for cp in self.remote:
            cp.wait_send()


def place_of():
    p, r, m = lax.axis_index("prefix"), lax.axis_index("resp"), lax.axis_index("mp")
    zl, y, x, c = p // 4, p % 4, r // 2, r % 2
    sib = {"resp": x * 2 + 1 - c}
    mate = {"mp": 1 - m}
    zmate = {"prefix": (1 - zl) * 4 + y}
    xs = [{"resp": ((x + d) % 4) * 2 + c} for d in (1, 2, 3)]
    ys = [{"prefix": zl * 4 + (y + d) % 4} for d in (1, 2, 3)]
    return zl, y, x, c, m, sib, mate, zmate, xs, ys


def meet(peers):
    barrier = pltpu.get_barrier_semaphore()
    for peer in peers:
        pl.semaphore_signal(barrier, inc=1, device_id=peer, device_id_type=MESH)
    pl.semaphore_wait(barrier, len(peers))


def bring_kernel(q, g, rkv, pkv, qh, gh, kv, send, recv, local):
    zl, y, x, c, m, sib, mate, zmate, xs, ys = place_of()
    mv = Mover(send, recv, local)
    own = []
    T2 = T // 2
    mine_r = x * 256 + c * 128
    own.append(mv.here(rkv.at[:, pl.ds(2 * m, 2)], kv.at[:, :, 2, :, pl.ds(mine_r + m * T2, T2)]))
    for a in range(2):
        own.append(mv.here(pkv.at[a], kv.at[a, :, 0:2, zl, pl.ds(y * 256, 256)]))
    meet([sib, mate, zmate] + xs + ys)
    b1 = mv.to(rkv.at[:, pl.ds(2 * (1 - m), 2)], kv.at[:, :, 2, :, pl.ds(mine_r + m * T2, T2)], mate)
    c1 = mv.to(pkv.at[c], kv.at[c, :, 0:2, zl, pl.ds(y * 256, 256)], zmate)
    c2a = [mv.to(pkv.at[c], kv.at[c, :, 0:2, zl, pl.ds(y * 256, 256)], w) for w in ys]
    swaps = []
    for b in range(2):
        for s, d in ((q, qh), (g, gh)):
            swaps.append(mv.to(s.at[b, :, pl.ds(16 * (1 - m), 16)], d.at[b, pl.ds(T2 * m, T2)], mate))
            own.append(mv.here(s.at[b, :, pl.ds(16 * m, 16)], d.at[b, pl.ds(T2 * m, T2)]))
    own[0].wait()
    b1.wait_recv()
    rblk = lambda xx: kv.at[:, :, 2, :, pl.ds(xx * 256 + c * 128, 128)]
    b2 = [mv.to(rblk(x), rblk(x), w) for w in xs]
    b3 = [mv.to(rblk(x), rblk(x), sib)]
    pblk = lambda z, yy: kv.at[c, :, 0:2, z, pl.ds(yy * 256, 256)]
    c1.wait_recv()
    c2b = [mv.to(pblk(1 - zl, y), pblk(1 - zl, y), w) for w in ys]
    c3 = [mv.to(pblk(1 - zl, y), pblk(1 - zl, y), sib)]
    for d in (0, 2, 1):
        yy, xx = (y + 3 - d) % 4, (x + 3 - d) % 4
        c2a[d].wait_recv()
        c3.append(mv.to(pblk(zl, yy), pblk(zl, yy), sib))
        b2[d].wait_recv()
        b3.append(mv.to(rblk(xx), rblk(xx), sib))
    for d in (0, 2, 1):
        yy = (y + 3 - d) % 4
        c2b[d].wait_recv()
        c3.append(mv.to(pblk(1 - zl, yy), pblk(1 - zl, yy), sib))
    for cp in b3 + c3 + swaps:
        cp.wait_recv()
    for cp in own[1:]:
        cp.wait()
    mv.drain()


def bring(q, g, rkv, pkv):
    return pl.pallas_call(
        bring_kernel,
        out_shape=[jax.ShapeDtypeStruct((2, T, 16, HD), BF)] * 2 + [jax.ShapeDtypeStruct((2, 2, 3, 2, 1024, HD), BF)],
        in_specs=[HBM] * 4,
        out_specs=[HBM] * 3,
        scratch_shapes=[pltpu.SemaphoreType.DMA((32,)), pltpu.SemaphoreType.DMA((32,)), pltpu.SemaphoreType.DMA((8,))],
        compiler_params=pltpu.CompilerParams(collective_id=1, has_side_effects=True),
    )(q, g, rkv, pkv)


def share_kernel(o, dq, terms, out, dout, fin, fr, far, s0, r1, s1, r2, s2, r3, rr1, rs, send, recv, local):
    zl, y, x, c, m, sib, mate, zmate, xs, ys = place_of()
    mv = Mover(send, recv, local)
    T2 = T // 2
    meet([sib, mate, zmate] + xs + ys)
    first = [mv.to(terms.at[1 - c, h], far.at[h], sib) for h in range(2)]
    own, swaps = [], []
    for b in range(2):
        for s, d in ((o, out), (dq, dout)):
            swaps.append(mv.to(s.at[b, pl.ds(T2 * (1 - m), T2)], d.at[b, :, pl.ds(16 * m, 16)], mate))
            own.append(mv.here(s.at[b, pl.ds(T2 * m, T2)], d.at[b, :, pl.ds(16 * m, 16)]))
    sent1, sentr = [], []
    for h in range(2):
        first[h].wait_recv()
        for i in range(3):
            for j in range(2):
                for k in range(4):
                    s0[h, i, j, k] = (terms[c, h, i, j, k].astype(F32) + far[h, i, j, k].astype(F32)).astype(BF)
        for d in range(3):
            if h == 0:
                part = s0.at[h, 0:2, :, :, (x + 1 + d) % 4]
            else:
                part = s0.at[h, 0:2, :, (y + 1 + d) % 4]
            sent1.append(mv.to(part, r1.at[h, d], xs[d] if h == 0 else ys[d]))
        for d in range(3):
            sentr.append(mv.to(s0.at[h, 2, :, (x + 1 + d) % 4], rr1.at[h, d], xs[d]))
    sent2 = []
    for h in range(2):
        for d in range(3):
            sent1[3 * h + d].wait_recv()
        for i in range(2):
            for j in range(2):
                for k in range(4):
                    a = s0[h, i, j, k, x] if h == 0 else s0[h, i, j, y, k]
                    t = a.astype(F32)
                    for d in range(3):
                        t = t + r1[h, d, i, j, k].astype(F32)
                    s1[h, i, j, k] = t.astype(BF)
        for d in range(3):
            at = (y if h == 0 else x) + 1 + d
            sent2.append(mv.to(s1.at[h, :, :, at % 4], r2.at[h, d], ys[d] if h == 0 else xs[d]))
    for d in range(6):
        sentr[d].wait_recv()
    for h in range(2):
        for b in range(2):
            for k in range(4):
                t = s0[h, 2, b, x, k].astype(F32)
                for d in range(3):
                    t = t + rr1[h, d, b, k].astype(F32)
                rs[c, h, b, k] = t.astype(BF)
    pair = mv.to(rs.at[c, :, :, pl.ds(2 * (1 - c), 2)], rs.at[c, :, :, pl.ds(2 * (1 - c), 2)], sib)
    sent3 = []
    for h in range(2):
        for d in range(3):
            sent2[3 * h + d].wait_recv()
        for i in range(2):
            for j in range(2):
                t = s1[h, i, j, y if h == 0 else x].astype(F32)
                for d in range(3):
                    t = t + r2[h, d, i, j].astype(F32)
                s2[h, i, j] = t.astype(BF)
        sent3.append(mv.to(s2.at[h, :, 1 - zl], r3.at[h], zmate))
    pair.wait_recv()
    mine = mv.here(rs.at[:, :, :, 2 * c + m], fr.at[:, pl.ds(2 * m, 2)])
    last = mv.to(rs.at[:, :, :, 2 * c + 1 - m], fr.at[:, pl.ds(2 * m, 2)], mate)
    for h in range(2):
        sent3[h].wait_recv()
        for i in range(2):
            fin[c, h, i, x] = (s2[h, i, zl].astype(F32) + r3[h, i].astype(F32)).astype(BF)
    spread = [mv.to(fin.at[c, :, :, x], fin.at[c, :, :, x], w) for w in xs]
    twin = [mv.to(fin.at[c, :, :, x], fin.at[c, :, :, x], sib)]
    for d in (0, 2, 1):
        spread[d].wait_recv()
        xx = (x + 3 - d) % 4
        twin.append(mv.to(fin.at[c, :, :, xx], fin.at[c, :, :, xx], sib))
    for cp in twin + swaps + [last]:
        cp.wait_recv()
    for cp in own + [mine]:
        cp.wait()
    mv.drain()


def share(o, dq, terms):
    v = pltpu.VMEM
    return pl.pallas_call(
        share_kernel,
        out_shape=[jax.ShapeDtypeStruct((2, T // 2, 32, HD), BF)] * 2
        + [jax.ShapeDtypeStruct((2, 2, 2, 4, 64, HD), BF), jax.ShapeDtypeStruct((2, 4, 2, 64, HD), BF)],
        in_specs=[HBM, HBM, VM],
        out_specs=[HBM, HBM, VM, VM],
        scratch_shapes=[
            v((2, 3, 2, 4, 4, 64, HD), BF), v((2, 3, 2, 4, 4, 64, HD), BF),
            v((2, 3, 2, 2, 4, 64, HD), BF), v((2, 2, 2, 4, 64, HD), BF),
            v((2, 3, 2, 2, 64, HD), BF), v((2, 2, 2, 64, HD), BF), v((2, 2, 64, HD), BF),
            v((2, 3, 2, 4, 64, HD), BF), v((2, 2, 2, 4, 64, HD), BF),
            pltpu.SemaphoreType.DMA((40,)), pltpu.SemaphoreType.DMA((40,)), pltpu.SemaphoreType.DMA((8,)),
        ],
        compiler_params=pltpu.CompilerParams(collective_id=2, has_side_effects=True, vmem_limit_bytes=48 * 2**20),
    )(o, dq, terms)


def per_device(queries, resp_keys, resp_values, prefix_keys, prefix_values, grad_out, prompt_ids, prefix_lengths, resp_lengths):
    rkv = jnp.stack([resp_keys, resp_values]).transpose(0, 3, 1, 2, 4)
    pkv = jnp.stack([prefix_keys, prefix_values]).transpose(0, 3, 1, 2, 4)
    q, g, kv = bring(queries, grad_out, rkv, pkv)
    kv = kv.reshape(2, 2, ROWS, HD)
    first = lax.axis_index("prefix") * 2
    prompts = lax.dynamic_slice_in_dim(prompt_ids, first, 2)
    lengths = lax.dynamic_slice_in_dim(resp_lengths, first, 2)
    pos0 = lax.axis_index("resp") * T
    meta = jnp.concatenate([pos0[None], prompts, lengths, prefix_lengths[prompts], jnp.zeros((1,), jnp.int32)]).astype(jnp.int32)
    o, dq, terms = attend()(meta, q, g, kv)
    attention, d_queries, fin, fr = share(o, dq, terms.reshape(2, 2, 3, 2, 4, 4, 64, HD))
    fin = fin.reshape(2, 2, 2, 256, HD).transpose(0, 2, 3, 1, 4)
    fr = fr.transpose(0, 2, 3, 1, 4)
    return (attention, d_queries, fr[0], fr[1], fin[0], fin[1])


def solution(mesh):
    rows = P("prefix", ("resp", "mp"), None, None)
    pre = P(None, "prefix", "mp", None)
    return jax.shard_map(
        per_device,
        mesh=mesh,
        in_specs=(rows, rows, rows, pre, pre, rows, P(), P(), P()),
        out_specs=(rows, rows, rows, rows, pre, pre),
        check_vma=False,
    )
```

```python
import math

import jax
import jax.numpy as jnp
from jax import lax
from jax.experimental import pallas as pl
from jax.experimental.pallas import tpu as pltpu
from jax.sharding import PartitionSpec as P

HD = 128
PRE = 2048
RL = 1024
T = 128
T2 = T // 2
G = 8
R = T * G
KB = 1024
RC = 256
NT = (((1,), (1,)), ((), ()))
NN = (((1,), (0,)), ((), ()))
TN = (((0,), (0,)), ((), ()))
MESH = pl.DeviceIdType.MESH
HBM = pl.BlockSpec(memory_space=pl.ANY)
VM = pl.BlockSpec(memory_space=pltpu.VMEM)
SM = pl.BlockSpec(memory_space=pltpu.SMEM)
BF = jnp.bfloat16
F32 = jnp.float32
INV = 1.0 / math.sqrt(HD)
C2 = math.log2(math.e) / math.sqrt(HD)


def dot(a, b, dims):
    return lax.dot_general(a, b, dims, preferred_element_type=F32)


class Mover:
    def __init__(self, send, recv, local):
        self.send, self.recv, self.local, self.n, self.m = send, recv, local, 0, 0
        self.remote = []

    def to(self, src, dst, where):
        cp = pltpu.make_async_remote_copy(
            src_ref=src, dst_ref=dst, send_sem=self.send.at[self.n], recv_sem=self.recv.at[self.n],
            device_id=where, device_id_type=MESH)
        self.n += 1
        cp.start()
        self.remote.append(cp)
        return cp

    def here(self, src, dst):
        cp = pltpu.make_async_copy(src, dst, self.local.at[self.m])
        self.m += 1
        cp.start()
        return cp

    def drain(self):
        for cp in self.remote:
            cp.wait_send()


def got(copies):
    for cp in copies:
        cp.wait_recv()


def kernel(pid, plen_ref, rlen_ref, q, g, rkv, pkv, out, dout, fin, fr,
           qb, gb, pk0, pv0, pre1, res, S, Pm, D, qhl, qr, dr, mx, ls, oacc, dqacc, X, oh, dqh, ob, dqb,
           tm, far, s0, r1, s1, r2, s2, r3, rr1, rs, send, recv, local):
    p, r, m = lax.axis_index("prefix"), lax.axis_index("resp"), lax.axis_index("mp")
    zl, y, x, c = p // 4, p % 4, r // 2, r % 2
    sib = {"resp": x * 2 + 1 - c}
    mate = {"mp": 1 - m}
    zmate = {"prefix": (1 - zl) * 4 + y}
    xs = [{"resp": ((x + d) % 4) * 2 + c} for d in (1, 2, 3)]
    ys = [{"prefix": zl * 4 + (y + d) % 4} for d in (1, 2, 3)]
    mv = Mover(send, recv, local)
    pos0 = r * T
    mine_r = r * T
    half = c * 128

    own_q = [[mv.here(s.at[b, :, pl.ds(16 * m, 16)], d.at[b, pl.ds(T2 * m, T2)]) for s, d in ((q, qb), (g, gb))] for b in range(2)]
    own_r = mv.here(rkv.at[:, pl.ds(2 * m, 2)], res.at[:, :, :, pl.ds(mine_r + m * T2, T2)])
    own_p = [mv.here(pkv.at[0, 0], pk0.at[:, zl, pl.ds(y * 256, 256)]), mv.here(pkv.at[1, 0], pv0.at[:, zl, pl.ds(y * 256, 256)]),
             mv.here(pkv.at[:, 1], pre1.at[:, :, zl, pl.ds(y * 256, 256)])]
    peers = [sib, mate, zmate] + xs + ys
    barrier = pltpu.get_barrier_semaphore()
    for peer in peers:
        pl.semaphore_signal(barrier, inc=1, device_id=peer, device_id_type=MESH)
    pl.semaphore_wait(barrier, len(peers))

    pk_at = lambda z, yy: pk0.at[:, z, pl.ds(yy * 256 + half, 128)]
    pv_at = lambda z, yy: pv0.at[:, z, pl.ds(yy * 256 + half, 128)]
    p1_at = lambda z, yy: pre1.at[:, :, z, pl.ds(yy * 256 + half, 128)]
    r_at = lambda h, xx: res.at[:, h, :, pl.ds(xx * 256 + c * 128, 128)]

    def swap_in(b, s, d):
        return mv.to(s.at[b, :, pl.ds(16 * (1 - m), 16)], d.at[b, pl.ds(T2 * m, T2)], mate)

    def spread_z(src, at):
        return mv.to(src, at(zl, y), zmate), [mv.to(src, at(zl, y), w) for w in ys]

    def pass_z(cp, at):
        cp.wait_recv()
        return [mv.to(at(1 - zl, y), at(1 - zl, y), w) for w in ys], [mv.to(at(1 - zl, y), at(1 - zl, y), sib)]

    def pass_y(near, other, at):
        sent = []
        for z, cps in ((zl, near), (1 - zl, other)):
            for d in (0, 2, 1):
                yy = (y + 3 - d) % 4
                cps[d].wait_recv()
                sent.append(mv.to(at(z, yy), at(z, yy), sib))
        return sent

    def spread_r(h):
        return [mv.to(r_at(h, x), r_at(h, x), w) for w in xs], [mv.to(r_at(h, x), r_at(h, x), sib)]

    def pass_r(cps):
        sent = []
        for d in (0, 2, 1):
            xx = (x + 3 - d) % 4
            cps[0][d].wait_recv()
            sent.append(mv.to(cps[2](xx), cps[2](xx), sib))
        return sent

    mine_p = lambda kv, h: pkv.at[kv, h, :, pl.ds(half, 128)]
    rz = mv.to(rkv.at[:, pl.ds(2 * (1 - m), 2)], res.at[:, :, :, pl.ds(mine_r + m * T2, T2)], mate)
    kz, ky = spread_z(mine_p(0, 0), pk_at)
    q_in = [swap_in(0, q, qb), None]
    vz, vy = spread_z(mine_p(1, 0), pv_at)
    g_in = [swap_in(0, g, gb), None]
    own_r.wait()
    rz.wait_recv()
    rx0, rs0 = spread_r(0)
    ky2, ks = pass_z(kz, pk_at)
    vy2, vs = pass_z(vz, pv_at)
    ks += pass_y(ky, ky2, pk_at)
    rs0 += pass_r((rx0, None, lambda xx: r_at(0, xx)))
    for cp in own_q[0] + own_p:
        cp.wait()
    got([q_in[0]] + rs0 + ks)

    def prefix_rows(h, kv, prompt, i):
        if h == 0:
            ref = pk0 if kv == 0 else pv0
            return ref[prompt, i]
        return pre1[kv, prompt, i]

    def limits(b, rc, resp):
        if not resp:
            return plen_ref[pid[2 * p + b]] - 1
        t = pos0 + rc // G + lax.broadcasted_iota(jnp.int32, (RC, 1), 0) // G
        return jnp.minimum(t, rlen_ref[2 * p + b] - 1)

    def head_rows(ref, b, h, rc):
        a = ref[b, pl.ds(rc // G, RC // G)].astype(F32)
        return a[:, h * G : (h + 1) * G].reshape(RC, HD)

    def pass_a(h, b):
        prompt = pid[2 * p + b]
        for rc in range(0, R, RC):
            rows = pl.ds(rc, RC)
            a = head_rows(qb, b, h, rc)
            qr[rows] = a.astype(BF)
            a = a * C2
            hi = a.astype(BF)
            qhl[rows, 0:HD] = hi
            qhl[rows, HD : 2 * HD] = (a - hi.astype(F32)).astype(BF)
        mx[...] = jnp.full_like(mx, -jnp.inf)

        def block(kb, col0, base, resp):
            kk = jnp.concatenate([kb, kb], axis=1)
            col = base + lax.broadcasted_iota(jnp.int32, (RC, KB), 1)
            for rc in range(0, R, RC):
                rows = pl.ds(rc, RC)
                s = dot(qhl[rows], kk, NT)
                s = jnp.where(col <= limits(b, rc, resp), s, -1e30)
                S[rows, pl.ds(col0, KB)] = s
                top = mx[rows]
                for k in range(0, KB, 128):
                    top = jnp.maximum(top, s[:, k : k + 128])
                mx[rows] = top

        def step(i, _):
            start = pl.multiple_of(i * KB, KB)
            block(prefix_rows(h, 0, prompt, i), start, start, False)
            return 0

        lax.fori_loop(0, PRE // KB, step, 0)
        block(res[0, h, b], PRE, 0, True)
        for rc in range(0, R, RC):
            rows = pl.ds(rc, RC)
            mx[rows] = jnp.broadcast_to(jnp.max(mx[rows], axis=1, keepdims=True), (RC, 128))

    def pass_b(h, b):
        prompt = pid[2 * p + b]
        ls[...] = jnp.zeros_like(ls)
        oacc[...] = jnp.zeros_like(oacc)

        def block(vb, col0):
            cols = pl.ds(col0, KB)
            for rc in range(0, R, RC):
                rows = pl.ds(rc, RC)
                top = mx[rows]
                s = S[rows, cols]
                total = ls[rows]
                parts = []
                for k in range(0, KB, 128):
                    e = jnp.exp2(s[:, k : k + 128] - top)
                    total = total + e
                    parts.append(e.astype(BF))
                ls[rows] = total
                pb = jnp.concatenate(parts, axis=1)
                Pm[rows, cols] = pb
                oacc[rows] += dot(pb, vb, NN)

        def step(i, _):
            block(prefix_rows(h, 1, prompt, i), pl.multiple_of(i * KB, KB))
            return 0

        lax.fori_loop(0, PRE // KB, step, 0)
        block(res[1, h, b], PRE)
        for rc in range(0, R, RC):
            rows = pl.ds(rc, RC)
            il = 1.0 / jnp.sum(ls[rows], axis=1, keepdims=True)
            o = (oacc[rows] * il).astype(BF).astype(F32)
            if h == 0:
                oh[b, rows] = o
            else:
                both = jnp.concatenate([oh[b, rows].reshape(RC // G, G, HD), o.reshape(RC // G, G, HD)], axis=1)
                ob[b, pl.ds(rc // G, RC // G)] = both.astype(BF)
            d = head_rows(gb, b, h, rc)
            t = pos0 + rc // G + lax.broadcasted_iota(jnp.int32, (RC, 1), 0) // G
            d = jnp.where(t < rlen_ref[2 * p + b], d, 0.0)
            delta = jnp.sum(d * o, axis=1, keepdims=True)
            dr[rows] = (d * il).astype(BF)
            mx[rows] = jnp.broadcast_to(delta * il, (RC, 128))

    def pass_c(h, b):
        prompt = pid[2 * p + b]
        dqacc[...] = jnp.zeros_like(dqacc)

        def block(kb, vb, col0):
            cols = pl.ds(col0, KB)
            for rc in range(0, R, RC):
                rows = pl.ds(rc, RC)
                dp = dot(dr[rows], vb, NT)
                e = Pm[rows, cols].astype(F32)
                dl = mx[rows]
                ds = jnp.concatenate([e[:, k : k + 128] * (dp[:, k : k + 128] - dl) for k in range(0, KB, 128)], axis=1).astype(BF)
                D[rows] = ds
                dqacc[rows] += dot(ds, kb, NN)
            dk = dot(qr[...], D[...], TN).T * INV
            dv = dot(dr[...], Pm[:, cols], TN).T
            return dk, dv

        def step(i, _):
            dkv = block(prefix_rows(h, 0, prompt, i), prefix_rows(h, 1, prompt, i), pl.multiple_of(i * KB, KB))
            for kv in range(2):
                if b == 0:
                    X[kv, i] = dkv[kv]
                else:
                    before = pid[2 * p]
                    for a in range(2):
                        e = jnp.where(before == a, X[kv, i], 0.0) + jnp.where(prompt == a, dkv[kv], 0.0)
                        tm[h, kv, a, i] = e.astype(BF).reshape(4, 4, 64, HD)
            return 0

        lax.fori_loop(0, PRE // KB, step, 0)
        dkv = block(res[0, h, b], res[1, h, b], PRE)
        for kv in range(2):
            tm[h, kv, 2, b] = dkv[kv].astype(BF).reshape(4, 4, 64, HD)
        for rc in range(0, R, RC):
            rows = pl.ds(rc, RC)
            e = dqacc[rows] * INV
            if h == 0:
                dqh[b, rows] = e
            else:
                both = jnp.concatenate([dqh[b, rows].reshape(RC // G, G, HD), e.reshape(RC // G, G, HD)], axis=1)
                dqb[b, pl.ds(rc // G, RC // G)] = both.astype(BF)

    ends = []

    def swap_out(b, s, d):
        ends.append(mv.to(s.at[b, pl.ds(T2 * (1 - m), T2)], d.at[b, :, pl.ds(16 * m, 16)], mate))
        owns.append(mv.here(s.at[b, pl.ds(T2 * m, T2)], d.at[b, :, pl.ds(16 * m, 16)]))

    owns = []

    def pair_sum(h, cp):
        cp.wait_recv()
        for i in range(3):
            for j in range(2):
                for k in range(4):
                    s0[h, i, j, k] = (tm[h, c, i, j, k].astype(F32) + far[h, i, j, k].astype(F32)).astype(BF)
        a = [mv.to(s0.at[h, 0, :, :, (x + 1 + d) % 4], r1.at[h, 0, d], xs[d]) for d in range(3)]
        b = [mv.to(s0.at[h, 1, :, (y + 1 + d) % 4], r1.at[h, 1, d], ys[d]) for d in range(3)]
        e = [mv.to(s0.at[h, 2, :, (x + 1 + d) % 4], rr1.at[h, d], xs[d]) for d in range(3)]
        return a, b, e

    def second(h, cps):
        sent = []
        for a in range(2):
            got(cps[a])
            for j in range(2):
                for k in range(4):
                    t = (s0[h, 0, j, k, x] if a == 0 else s0[h, 1, j, y, k]).astype(F32)
                    for d in range(3):
                        t = t + r1[h, a, d, j, k].astype(F32)
                    s1[h, a, j, k] = t.astype(BF)
            at = y if a == 0 else x
            sent.append([mv.to(s1.at[h, a, :, (at + 1 + d) % 4], r2.at[h, a, d], (ys if a == 0 else xs)[d]) for d in range(3)])
        return sent

    def resp_sum(h, cps):
        got(cps[2])
        for b in range(2):
            for k in range(4):
                t = s0[h, 2, b, x, k].astype(F32)
                for d in range(3):
                    t = t + rr1[h, d, b, k].astype(F32)
                rs[c, h, b, k] = t.astype(BF)
        at = rs.at[c, h, :, pl.ds(2 * (1 - c), 2)]
        return mv.to(at, at, sib)

    def resp_out(h, cp):
        cp.wait_recv()
        owns.append(mv.here(rs.at[:, h, :, 2 * c + m], fr.at[:, 2 * m + h]))
        ends.append(mv.to(rs.at[:, h, :, 2 * c + 1 - m], fr.at[:, 2 * m + h], mate))

    def third(h, cps):
        for a in range(2):
            got(cps[a])
            for j in range(2):
                t = s1[h, a, j, y if a == 0 else x].astype(F32)
                for d in range(3):
                    t = t + r2[h, a, d, j].astype(F32)
                s2[h, a, j] = t.astype(BF)
        return mv.to(s2.at[h, :, 1 - zl], r3.at[h], zmate)

    def final(h, cp):
        cp.wait_recv()
        for a in range(2):
            fin[c, h, a, x] = (s2[h, a, zl].astype(F32) + r3[h, a].astype(F32)).astype(BF)
        at = fin.at[c, h, :, x]
        ends.append(mv.to(at, at, sib))
        return [mv.to(at, at, w) for w in xs]

    def twin(h, cps):
        for d in (0, 2, 1):
            cps[d].wait_recv()
            at = fin.at[c, h, :, (x + 3 - d) % 4]
            ends.append(mv.to(at, at, sib))

    pass_a(0, 0)
    vs += pass_y(vy, vy2, pv_at)
    q_in[1], g_in[1] = swap_in(1, q, qb), swap_in(1, g, gb)
    pz, py = spread_z(pkv.at[:, 1, :, pl.ds(half, 128)], p1_at)
    rx1, rs1 = spread_r(1)
    got([g_in[0]] + vs)
    pass_b(0, 0)
    pass_c(0, 0)
    py2, ps = pass_z(pz, p1_at)
    rs1 += pass_r((rx1, None, lambda xx: r_at(1, xx)))
    for cp in own_q[1]:
        cp.wait()
    got([q_in[1], g_in[1]])
    pass_a(0, 1)
    ps += pass_y(py, py2, p1_at)
    pass_b(0, 1)
    pass_c(0, 1)
    first0 = mv.to(tm.at[0, 1 - c], far.at[0], sib)
    got(ps + rs1)
    pass_a(1, 0)
    a0 = pair_sum(0, first0)
    pass_b(1, 0)
    swap_out(0, ob, out)
    pass_c(1, 0)
    swap_out(0, dqb, dout)
    b0 = second(0, a0)
    e0 = resp_sum(0, a0)
    pass_a(1, 1)
    z0 = third(0, b0)
    resp_out(0, e0)
    pass_b(1, 1)
    swap_out(1, ob, out)
    f0 = final(0, z0)
    pass_c(1, 1)
    first1 = mv.to(tm.at[1, 1 - c], far.at[1], sib)
    swap_out(1, dqb, dout)
    twin(0, f0)
    a1 = pair_sum(1, first1)
    b1 = second(1, a1)
    e1 = resp_sum(1, a1)
    z1 = third(1, b1)
    resp_out(1, e1)
    f1 = final(1, z1)
    twin(1, f1)
    got(ends)
    for cp in owns:
        cp.wait()
    mv.drain()


def fused(pid, plens, rlens, q, g, rkv, pkv):
    v = pltpu.VMEM
    n = 128
    return pl.pallas_call(
        kernel,
        out_shape=[jax.ShapeDtypeStruct((2, T2, 32, HD), BF)] * 2
        + [jax.ShapeDtypeStruct((2, 2, 2, 4, 64, HD), BF), jax.ShapeDtypeStruct((2, 4, 2, 64, HD), BF)],
        in_specs=[SM] * 3 + [HBM] * 4,
        out_specs=[HBM, HBM, VM, VM],
        scratch_shapes=[
            v((2, T, 16, HD), BF), v((2, T, 16, HD), BF),
            v((2, 2, 1024, HD), BF), v((2, 2, 1024, HD), BF), v((2, 2, 2, 1024, HD), BF), v((2, 2, 2, 1024, HD), BF),
            v((R, PRE + RL), F32), v((R, PRE + RL), BF), v((R, KB), BF),
            v((R, 2 * HD), BF), v((R, HD), BF), v((R, HD), BF),
            v((R, 128), F32), v((R, 128), F32), v((R, HD), F32), v((R, HD), F32),
            v((2, 2, 1024, HD), F32), v((2, R, HD), F32), v((2, R, HD), F32), v((2, T, 16, HD), BF), v((2, T, 16, HD), BF),
            v((2, 2, 3, 2, 4, 4, 64, HD), BF), v((2, 3, 2, 4, 4, 64, HD), BF), v((2, 3, 2, 4, 4, 64, HD), BF),
            v((2, 2, 3, 2, 4, 64, HD), BF), v((2, 2, 2, 4, 64, HD), BF),
            v((2, 2, 3, 2, 64, HD), BF), v((2, 2, 2, 64, HD), BF), v((2, 2, 64, HD), BF),
            v((2, 3, 2, 4, 64, HD), BF), v((2, 2, 2, 4, 64, HD), BF),
            pltpu.SemaphoreType.DMA((n,)), pltpu.SemaphoreType.DMA((n,)), pltpu.SemaphoreType.DMA((32,)),
        ],
        compiler_params=pltpu.CompilerParams(collective_id=1, has_side_effects=True, vmem_limit_bytes=62 * 2**20),
    )(pid, plens, rlens, q, g, rkv, pkv)


def per_device(queries, resp_keys, resp_values, prefix_keys, prefix_values, grad_out, prompt_ids, prefix_lengths, resp_lengths):
    rkv = jnp.stack([resp_keys, resp_values]).transpose(0, 3, 1, 2, 4)
    pkv = jnp.stack([prefix_keys, prefix_values]).transpose(0, 3, 1, 2, 4)
    attention, d_queries, fin, fr = fused(prompt_ids, prefix_lengths, resp_lengths, queries, grad_out, rkv, pkv)
    fin = fin.reshape(2, 2, 2, 256, HD).transpose(0, 2, 3, 1, 4)
    fr = fr.transpose(0, 2, 3, 1, 4)
    return (attention, d_queries, fr[0], fr[1], fin[0], fin[1])


def solution(mesh):
    rows = P("prefix", ("resp", "mp"), None, None)
    pre = P(None, "prefix", "mp", None)
    return jax.shard_map(
        per_device,
        mesh=mesh,
        in_specs=(rows, rows, rows, pre, pre, rows, P(), P(), P()),
        out_specs=(rows, rows, rows, rows, pre, pre),
        check_vma=False,
    )
```

```python
import math

import jax
import jax.numpy as jnp
from jax import lax
from jax.experimental import pallas as pl
from jax.experimental.pallas import tpu as pltpu
from jax.sharding import PartitionSpec as P

HD = 128
PRE = 2048
RL = 1024
T = 128
T2 = T // 2
G = 8
R = T * G
KB = 1024
RC = 256
NT = (((1,), (1,)), ((), ()))
NN = (((1,), (0,)), ((), ()))
TN = (((0,), (0,)), ((), ()))
MESH = pl.DeviceIdType.MESH
HBM = pl.BlockSpec(memory_space=pl.ANY)
VM = pl.BlockSpec(memory_space=pltpu.VMEM)
SM = pl.BlockSpec(memory_space=pltpu.SMEM)
BF = jnp.bfloat16
F32 = jnp.float32
INV = 1.0 / math.sqrt(HD)
C2 = math.log2(math.e) / math.sqrt(HD)


def dot(a, b, dims):
    return lax.dot_general(a, b, dims, preferred_element_type=F32)


class Mover:
    def __init__(self, send, recv, local):
        self.send, self.recv, self.local, self.n, self.m = send, recv, local, 0, 0
        self.remote = []

    def to(self, src, dst, where):
        cp = pltpu.make_async_remote_copy(
            src_ref=src, dst_ref=dst, send_sem=self.send.at[self.n], recv_sem=self.recv.at[self.n],
            device_id=where, device_id_type=MESH)
        self.n += 1
        cp.start()
        self.remote.append(cp)
        return cp

    def here(self, src, dst):
        cp = pltpu.make_async_copy(src, dst, self.local.at[self.m])
        self.m += 1
        cp.start()
        return cp

    def drain(self):
        for cp in self.remote:
            cp.wait_send()


def got(copies):
    for cp in copies:
        cp.wait_recv()


def kernel(pid, plen_ref, rlen_ref, q, g, rkv, pkv, out, dout, fin, fr,
           qb, gb, pk0, pv0, pre1, res, S, Pm, D, qhl, qr, dr, mx, ls, oacc, dqacc, X, oh, dqh, ob, dqb,
           tm, far, s0, r1, s1, r2, rr1, rs, send, recv, local):
    p, r, m = lax.axis_index("prefix"), lax.axis_index("resp"), lax.axis_index("mp")
    zl, y, x, c = p // 4, p % 4, r // 2, r % 2
    sib = {"resp": x * 2 + 1 - c}
    mate = {"mp": 1 - m}
    zmate = {"prefix": (1 - zl) * 4 + y}
    xs = [{"resp": ((x + d) % 4) * 2 + c} for d in (1, 2, 3)]
    ys = [{"prefix": zl * 4 + (y + d) % 4} for d in (1, 2, 3)]
    cross = {"resp": x * 2 + 1 - c, "mp": 1 - m}
    zy = [{"prefix": ((zl + dz) % 2) * 4 + (y + d) % 4} for dz in range(2) for d in range(4)][1:]
    zx = [{"prefix": ((zl + dz) % 2) * 4 + y, "resp": ((x + d) % 4) * 2 + c} for dz in range(2) for d in range(4)][1:]
    xc = [{"resp": ((x + d) % 4) * 2 + (c + dc) % 2} for dc in range(2) for d in range(4)][1:]
    mv = Mover(send, recv, local)
    pos0 = r * T
    mine_r = r * T
    half = c * 128

    own_q = [[mv.here(s.at[b, :, pl.ds(16 * m, 16)], d.at[b, pl.ds(T2 * m, T2)]) for s, d in ((q, qb), (g, gb))] for b in range(2)]
    own_r = mv.here(rkv.at[:, pl.ds(2 * m, 2)], res.at[:, :, :, pl.ds(mine_r + m * T2, T2)])
    own_p = [mv.here(pkv.at[0, 0], pk0.at[:, zl, pl.ds(y * 256, 256)]), mv.here(pkv.at[1, 0], pv0.at[:, zl, pl.ds(y * 256, 256)]),
             mv.here(pkv.at[:, 1], pre1.at[:, :, zl, pl.ds(y * 256, 256)])]
    peers = [mate, cross] + zy + [zx[k] for k in (4, 5, 6)] + xc
    barrier = pltpu.get_barrier_semaphore()
    for peer in peers:
        pl.semaphore_signal(barrier, inc=1, device_id=peer, device_id_type=MESH)
    pl.semaphore_wait(barrier, len(peers))

    pk_at = lambda z, yy: pk0.at[:, z, pl.ds(yy * 256 + half, 128)]
    pv_at = lambda z, yy: pv0.at[:, z, pl.ds(yy * 256 + half, 128)]
    p1_at = lambda z, yy: pre1.at[:, :, z, pl.ds(yy * 256 + half, 128)]
    r_at = (lambda xx: res.at[:, 0, 0, pl.ds(xx * 256 + half, 128)], lambda xx: res.at[:, 1, 0, pl.ds(xx * 256 + half, 128)],
            lambda xx: res.at[:, :, 1, pl.ds(xx * 256 + half, 128)])

    def swap_in(b, s, d):
        return mv.to(s.at[b, :, pl.ds(16 * (1 - m), 16)], d.at[b, pl.ds(T2 * m, T2)], mate)

    def swap_r(b):
        return mv.to(rkv.at[:, pl.ds(2 * (1 - m), 2), b], res.at[:, :, b, pl.ds(mine_r + m * T2, T2)], mate)

    def spread_y(src, at):
        return [mv.to(src, at(zl, y), w) for w in ys]

    def pass_z(cp, at):
        cp.wait_recv()
        return [mv.to(at(1 - zl, y), at(1 - zl, y), w) for w in ys], [mv.to(at(1 - zl, y), at(1 - zl, y), sib)]

    def pass_y(z, cps, at):
        sent = []
        for d in (0, 2, 1):
            yy = (y + 3 - d) % 4
            cps[d].wait_recv()
            sent.append(mv.to(at(z, yy), at(z, yy), sib))
        return sent

    def spread_r(u):
        at = r_at[u](x)
        return [mv.to(at, at, w) for w in xs], [mv.to(at, at, sib)]

    def pass_r(u, cps):
        sent = []
        for d in (0, 2, 1):
            cps[d].wait_recv()
            at = r_at[u]((x + 3 - d) % 4)
            sent.append(mv.to(at, at, sib))
        return sent

    mine_p = lambda kv, h: pkv.at[kv, h, :, pl.ds(half, 128)]
    mine_1 = pkv.at[:, 1, :, pl.ds(half, 128)]
    kz = mv.to(mine_p(0, 0), pk_at(zl, y), zmate)
    ky = spread_y(mine_p(0, 0), pk_at)
    rz0 = swap_r(0)
    q_in = [swap_in(0, q, qb), None]
    vz = mv.to(mine_p(1, 0), pv_at(zl, y), zmate)
    own_r.wait()
    ky2, ks = pass_z(kz, pk_at)
    vy = spread_y(mine_p(1, 0), pv_at)
    rz0.wait_recv()
    rx0, rs0 = spread_r(0)
    vy2, vs = pass_z(vz, pv_at)
    ks += pass_y(zl, ky, pk_at)
    pz = mv.to(mine_1, p1_at(zl, y), zmate)
    ks += pass_y(1 - zl, ky2, pk_at)
    for cp in own_q[0] + own_p:
        cp.wait()
    got([q_in[0]])
    g_in = [swap_in(0, g, gb), None]
    rx1, rs1 = spread_r(1)
    got(ks)

    def prefix_rows(h, kv, prompt, i):
        if h == 0:
            ref = pk0 if kv == 0 else pv0
            return ref[prompt, i]
        return pre1[kv, prompt, i]

    def limits(b, rc, resp):
        if not resp:
            return plen_ref[pid[2 * p + b]] - 1
        t = pos0 + rc // G + lax.broadcasted_iota(jnp.int32, (RC, 1), 0) // G
        return jnp.minimum(t, rlen_ref[2 * p + b] - 1)

    def head_rows(ref, b, h, rc):
        a = ref[b, pl.ds(rc // G, RC // G)].astype(F32)
        return a[:, h * G : (h + 1) * G].reshape(RC, HD)

    def pass_a(h, b, before_resp=None):
        prompt = pid[2 * p + b]
        for rc in range(0, R, RC):
            rows = pl.ds(rc, RC)
            a = head_rows(qb, b, h, rc)
            qr[rows] = a.astype(BF)
            a = a * C2
            hi = a.astype(BF)
            qhl[rows, 0:HD] = hi
            qhl[rows, HD : 2 * HD] = (a - hi.astype(F32)).astype(BF)
        mx[...] = jnp.full_like(mx, -jnp.inf)

        def block(kb, col0, base, resp):
            kk = jnp.concatenate([kb, kb], axis=1)
            col = base + lax.broadcasted_iota(jnp.int32, (RC, KB), 1)
            for rc in range(0, R, RC):
                rows = pl.ds(rc, RC)
                s = dot(qhl[rows], kk, NT)
                s = jnp.where(col <= limits(b, rc, resp), s, -1e30)
                S[rows, pl.ds(col0, KB)] = s
                top = mx[rows]
                for k in range(0, KB, 128):
                    top = jnp.maximum(top, s[:, k : k + 128])
                mx[rows] = top

        def step(i, _):
            start = pl.multiple_of(i * KB, KB)
            block(prefix_rows(h, 0, prompt, i), start, start, False)
            return 0

        lax.fori_loop(0, PRE // KB, step, 0)
        if before_resp is not None:
            before_resp()
        block(res[0, h, b], PRE, 0, True)
        for rc in range(0, R, RC):
            rows = pl.ds(rc, RC)
            mx[rows] = jnp.broadcast_to(jnp.max(mx[rows], axis=1, keepdims=True), (RC, 128))

    def pass_b(h, b):
        prompt = pid[2 * p + b]
        ls[...] = jnp.zeros_like(ls)
        oacc[...] = jnp.zeros_like(oacc)

        def block(vb, col0):
            cols = pl.ds(col0, KB)
            for rc in range(0, R, RC):
                rows = pl.ds(rc, RC)
                top = mx[rows]
                s = S[rows, cols]
                total = ls[rows]
                parts = []
                for k in range(0, KB, 128):
                    e = jnp.exp2(s[:, k : k + 128] - top)
                    total = total + e
                    parts.append(e.astype(BF))
                ls[rows] = total
                pb = jnp.concatenate(parts, axis=1)
                Pm[rows, cols] = pb
                oacc[rows] += dot(pb, vb, NN)

        def step(i, _):
            block(prefix_rows(h, 1, prompt, i), pl.multiple_of(i * KB, KB))
            return 0

        lax.fori_loop(0, PRE // KB, step, 0)
        block(res[1, h, b], PRE)
        for rc in range(0, R, RC):
            rows = pl.ds(rc, RC)
            il = 1.0 / jnp.sum(ls[rows], axis=1, keepdims=True)
            o = (oacc[rows] * il).astype(BF).astype(F32)
            if h == 0:
                oh[b, rows] = o
            else:
                both = jnp.concatenate([oh[b, rows].reshape(RC // G, G, HD), o.reshape(RC // G, G, HD)], axis=1)
                ob[b, pl.ds(rc // G, RC // G)] = both.astype(BF)
            d = head_rows(gb, b, h, rc)
            t = pos0 + rc // G + lax.broadcasted_iota(jnp.int32, (RC, 1), 0) // G
            d = jnp.where(t < rlen_ref[2 * p + b], d, 0.0)
            delta = jnp.sum(d * o, axis=1, keepdims=True)
            dr[rows] = (d * il).astype(BF)
            mx[rows] = jnp.broadcast_to(delta * il, (RC, 128))

    def pass_c(h, b, hooks=()):
        prompt = pid[2 * p + b]
        dqacc[...] = jnp.zeros_like(dqacc)

        def block(kb, vb, col0):
            cols = pl.ds(col0, KB)
            for rc in range(0, R, RC):
                rows = pl.ds(rc, RC)
                dp = dot(dr[rows], vb, NT)
                e = Pm[rows, cols].astype(F32)
                dl = mx[rows]
                ds = jnp.concatenate([e[:, k : k + 128] * (dp[:, k : k + 128] - dl) for k in range(0, KB, 128)], axis=1).astype(BF)
                D[rows] = ds
                dqacc[rows] += dot(ds, kb, NN)
            dk = dot(qr[...], D[...], TN).T * INV
            dv = dot(dr[...], Pm[:, cols], TN).T
            return dk, dv

        def step(i, _):
            dkv = block(prefix_rows(h, 0, prompt, i), prefix_rows(h, 1, prompt, i), i * KB if isinstance(i, int) else pl.multiple_of(i * KB, KB))
            for kv in range(2):
                if b == 0:
                    X[h, kv, i] = dkv[kv]
                else:
                    before = pid[2 * p]
                    for a in range(2):
                        e = jnp.where(before == a, X[h, kv, i], 0.0) + jnp.where(prompt == a, dkv[kv], 0.0)
                        tm[h, kv, a, i] = e.astype(BF).reshape(4, 4, 64, HD)
            return 0

        dkv = block(res[0, h, b], res[1, h, b], PRE)
        for kv in range(2):
            tm[h, kv, 2, b] = dkv[kv].astype(BF).reshape(4, 4, 64, HD)
        if hooks:
            for i in range(PRE // KB):
                hooks[i]()
                step(i, 0)
        else:
            lax.fori_loop(0, PRE // KB, step, 0)
        for rc in range(0, R, RC):
            rows = pl.ds(rc, RC)
            e = dqacc[rows] * INV
            if h == 0:
                dqh[b, rows] = e
            else:
                both = jnp.concatenate([dqh[b, rows].reshape(RC // G, G, HD), e.reshape(RC // G, G, HD)], axis=1)
                dqb[b, pl.ds(rc // G, RC // G)] = both.astype(BF)

    ends = []

    def swap_out(b, s, d):
        ends.append(mv.to(s.at[b, pl.ds(T2 * (1 - m), T2)], d.at[b, :, pl.ds(16 * m, 16)], mate))
        owns.append(mv.here(s.at[b, pl.ds(T2 * m, T2)], d.at[b, :, pl.ds(16 * m, 16)]))

    owns = []

    def trade(h, u):
        return mv.to(tm.at[h, 1 - c, 0:2, u], far.at[h, 0:2, u], sib)

    def pair_sum(h, u, cp):
        cp.wait_recv()
        for i in range(2):
            for k in range(4):
                s0[h, i, u, k] = (tm[h, c, i, u, k].astype(F32) + far[h, i, u, k].astype(F32)).astype(BF)
        return ([mv.to(s0.at[h, 0, u, :, (x + 1 + d) % 4], r1.at[h, 0, d, u], xs[d]) for d in range(3)],
                [mv.to(s0.at[h, 1, u, (y + 1 + d) % 4], r1.at[h, 1, d, u], ys[d]) for d in range(3)])

    def second(h, cps):
        sent = []
        for a in range(2):
            for j in range(2):
                got(cps[j][a])
                for k in range(4):
                    t = (s0[h, 0, j, k, x] if a == 0 else s0[h, 1, j, y, k]).astype(F32)
                    for d in range(3):
                        t = t + r1[h, a, d, j, k].astype(F32)
                    s1[h, a, j, k] = t.astype(BF)
            at = y if a == 0 else x
            for n in range(1, 8):
                sent.append(mv.to(s1.at[h, a, (zl + n // 4) % 2, (at + n % 4) % 4], r2.at[h, a, n - 1], (zy if a == 0 else zx)[n - 1]))
        return sent

    def final(h, cps):
        got(cps)
        for a in range(2):
            t = s1[h, a, zl, y if a == 0 else x].astype(F32)
            for n in range(7):
                t = t + r2[h, a, n].astype(F32)
            fin[c, h, a, x] = t.astype(BF)
        at = fin.at[c, h, :, x]
        ends.extend([mv.to(at, at, w) for w in xc])

    def trade_r(h, b):
        return mv.to(tm.at[h, 1 - c, 2, b], far.at[h, 2, b], sib)

    def pair_sum_r(h, b, cp):
        cp.wait_recv()
        for k in range(4):
            s0[h, 2, b, k] = (tm[h, c, 2, b, k].astype(F32) + far[h, 2, b, k].astype(F32)).astype(BF)
        return [mv.to(s0.at[h, 2, b, (x + 1 + d) % 4], rr1.at[h, d, b], xs[d]) for d in range(3)]

    def final_r(h, b, cps):
        got(cps)
        for k in range(4):
            t = s0[h, 2, b, x, k].astype(F32)
            for d in range(3):
                t = t + rr1[h, d, b, k].astype(F32)
            rs[h, b, k] = t.astype(BF)
        at = fr.at[c, 2 * m + h, b]
        owns.append(mv.here(rs.at[h, b, 2 * c + m], at))
        for core, part, w in ((1 - c, m, sib), (c, 1 - m, mate), (1 - c, 1 - m, cross)):
            ends.append(mv.to(rs.at[h, b, 2 * core + part], at, w))

    def resp_here():
        got(rs0 + pass_r(0, rx0))

    pass_a(0, 0, resp_here)
    vs += pass_y(zl, vy, pv_at)
    py = spread_y(mine_1, p1_at)
    py2, ps = pass_z(pz, p1_at)
    vs += pass_y(1 - zl, vy2, pv_at)
    rz1 = swap_r(1)
    got([g_in[0]] + vs)
    q_in[1] = swap_in(1, q, qb)
    pass_b(0, 0)
    ps += pass_y(zl, py, p1_at)
    rs1 += pass_r(1, rx1)
    got([rz1])
    rx2, rs2 = spread_r(2)
    pass_c(0, 0)
    t00 = trade_r(0, 0)
    g_in[1] = swap_in(1, g, gb)
    ps += pass_y(1 - zl, py2, p1_at)
    got(ps + rs1)
    pass_a(1, 0)
    t00 = pair_sum_r(0, 0, t00)
    rs2 += pass_r(2, rx2)
    pass_b(1, 0)
    swap_out(0, ob, out)
    pass_c(1, 0)
    t10 = trade_r(1, 0)
    swap_out(0, dqb, dout)
    final_r(0, 0, t00)
    for cp in own_q[1]:
        cp.wait()
    got(q_in[1:] + g_in[1:] + rs2)
    pass_a(0, 1)
    t10 = pair_sum_r(1, 0, t10)
    pass_b(0, 1)
    pass_c(0, 1)
    a0 = [trade(0, 0), trade(0, 1)]
    t01 = trade_r(0, 1)
    final_r(1, 0, t10)
    pass_a(1, 1)
    a0 = [pair_sum(0, u, a0[u]) for u in range(2)]
    t01 = pair_sum_r(0, 1, t01)
    pass_b(1, 1)
    swap_out(1, ob, out)
    b0 = second(0, a0)
    t11, a1 = [None], [None, None]

    def after_resp():
        t11[0] = trade_r(1, 1)
        final_r(0, 1, t01)

    def after_first():
        a1[0] = trade(1, 0)
        t11[0] = pair_sum_r(1, 1, t11[0])
        final(0, b0)

    pass_c(1, 1, (after_resp, after_first))
    a1[1] = trade(1, 1)
    swap_out(1, dqb, dout)
    a1[0] = pair_sum(1, 0, a1[0])
    a1[1] = pair_sum(1, 1, a1[1])
    final_r(1, 1, t11[0])
    final(1, second(1, a1))
    got(ends)
    for cp in owns:
        cp.wait()
    mv.drain()


def fused(pid, plens, rlens, q, g, rkv, pkv):
    v = pltpu.VMEM
    n = 200
    return pl.pallas_call(
        kernel,
        out_shape=[jax.ShapeDtypeStruct((2, T2, 32, HD), BF)] * 2
        + [jax.ShapeDtypeStruct((2, 2, 2, 4, 64, HD), BF), jax.ShapeDtypeStruct((2, 4, 2, 64, HD), BF)],
        in_specs=[SM] * 3 + [HBM] * 4,
        out_specs=[HBM, HBM, VM, VM],
        scratch_shapes=[
            v((2, T, 16, HD), BF), v((2, T, 16, HD), BF),
            v((2, 2, 1024, HD), BF), v((2, 2, 1024, HD), BF), v((2, 2, 2, 1024, HD), BF), v((2, 2, 2, 1024, HD), BF),
            v((R, PRE + RL), F32), v((R, PRE + RL), BF), v((R, KB), BF),
            v((R, 2 * HD), BF), v((R, HD), BF), v((R, HD), BF),
            v((R, 128), F32), v((R, 128), F32), v((R, HD), F32), v((R, HD), F32),
            v((2, 2, 2, 1024, HD), F32), v((2, R, HD), F32), v((2, R, HD), F32), v((2, T, 16, HD), BF), v((2, T, 16, HD), BF),
            v((2, 2, 3, 2, 4, 4, 64, HD), BF), v((2, 3, 2, 4, 4, 64, HD), BF), v((2, 3, 2, 4, 4, 64, HD), BF),
            v((2, 2, 3, 2, 4, 64, HD), BF), v((2, 2, 2, 4, 64, HD), BF),
            v((2, 2, 7, 64, HD), BF), v((2, 3, 2, 4, 64, HD), BF), v((2, 2, 4, 64, HD), BF),
            pltpu.SemaphoreType.DMA((n,)), pltpu.SemaphoreType.DMA((n,)), pltpu.SemaphoreType.DMA((32,)),
        ],
        compiler_params=pltpu.CompilerParams(collective_id=1, has_side_effects=True, vmem_limit_bytes=62 * 2**20),
    )(pid, plens, rlens, q, g, rkv, pkv)


def per_device(queries, resp_keys, resp_values, prefix_keys, prefix_values, grad_out, prompt_ids, prefix_lengths, resp_lengths):
    rkv = jnp.stack([resp_keys, resp_values]).transpose(0, 3, 1, 2, 4)
    pkv = jnp.stack([prefix_keys, prefix_values]).transpose(0, 3, 1, 2, 4)
    attention, d_queries, fin, fr = fused(prompt_ids, prefix_lengths, resp_lengths, queries, grad_out, rkv, pkv)
    fin = [fin[kv].reshape(2, 2, 256, HD).transpose(1, 2, 0, 3) for kv in range(2)]
    fr = [fr[kv].transpose(1, 2, 0, 3) for kv in range(2)]
    return (attention, d_queries, fr[0], fr[1], fin[0], fin[1])


def solution(mesh):
    rows = P("prefix", ("resp", "mp"), None, None)
    pre = P(None, "prefix", "mp", None)
    return jax.shard_map(
        per_device,
        mesh=mesh,
        in_specs=(rows, rows, rows, pre, pre, rows, P(), P(), P()),
        out_specs=(rows, rows, rows, rows, pre, pre),
        check_vma=False,
    )
```

```python
import math

import jax
import jax.numpy as jnp
from jax import lax
from jax.experimental import pallas as pl
from jax.experimental.pallas import tpu as pltpu
from jax.sharding import PartitionSpec as P

HD = 128
PRE = 2048
RL = 1024
T = 128
T2 = T // 2
G = 8
R = T * G
KB = 1024
RC = 256
NT = (((1,), (1,)), ((), ()))
NN = (((1,), (0,)), ((), ()))
TN = (((0,), (0,)), ((), ()))
MESH = pl.DeviceIdType.MESH
HBM = pl.BlockSpec(memory_space=pl.ANY)
VM = pl.BlockSpec(memory_space=pltpu.VMEM)
SM = pl.BlockSpec(memory_space=pltpu.SMEM)
BF = jnp.bfloat16
F32 = jnp.float32
INV = 1.0 / math.sqrt(HD)
C2 = math.log2(math.e) / math.sqrt(HD)


def dot(a, b, dims):
    return lax.dot_general(a, b, dims, preferred_element_type=F32)


class Mover:
    def __init__(self, send, recv, local):
        self.send, self.recv, self.local, self.n, self.m = send, recv, local, 0, 0
        self.remote = []

    def to(self, src, dst, where):
        cp = pltpu.make_async_remote_copy(
            src_ref=src, dst_ref=dst, send_sem=self.send.at[self.n], recv_sem=self.recv.at[self.n],
            device_id=where, device_id_type=MESH)
        self.n += 1
        cp.start()
        self.remote.append(cp)
        return cp

    def here(self, src, dst):
        cp = pltpu.make_async_copy(src, dst, self.local.at[self.m])
        self.m += 1
        cp.start()
        return cp

    def drain(self):
        for cp in self.remote:
            cp.wait_send()


def got(copies):
    for cp in copies:
        cp.wait_recv()


def kernel(pid, plen_ref, rlen_ref, q, g, rk, rv, pk, pv, out, dout, fin_k, fin_v, fr_k, fr_v,
           qb, gb, pk0, pv0, pre1, res, S, Pm, qhl, qr, dr, mx, ls, oacc, dqacc, X, oh, dqh, ob, dqb,
           tm, far, s0, r1, s1, r2, rr1, rs, fin, fr, send, recv, local):
    p, r, m = lax.axis_index("prefix"), lax.axis_index("resp"), lax.axis_index("mp")
    zl, y, x, c = p // 4, p % 4, r // 2, r % 2
    sib = {"resp": x * 2 + 1 - c}
    mate = {"mp": 1 - m}
    zmate = {"prefix": (1 - zl) * 4 + y}
    xs = [{"resp": ((x + d) % 4) * 2 + c} for d in (1, 2, 3)]
    ys = [{"prefix": zl * 4 + (y + d) % 4} for d in (1, 2, 3)]
    cross = {"resp": x * 2 + 1 - c, "mp": 1 - m}
    zy = [{"prefix": ((zl + dz) % 2) * 4 + (y + d) % 4} for dz in range(2) for d in range(4)][1:]
    zx = [{"prefix": ((zl + dz) % 2) * 4 + y, "resp": ((x + d) % 4) * 2 + c} for dz in range(2) for d in range(4)][1:]
    xc = [{"resp": ((x + d) % 4) * 2 + (c + dc) % 2} for dc in range(2) for d in range(4)][1:]
    mv = Mover(send, recv, local)
    pos0 = r * T
    mine_r = r * T
    half = c * 128

    own_q = [[mv.here(s.at[b, :, pl.ds(16 * m, 16)], d.at[b, pl.ds(T2 * m, T2)]) for s, d in ((q, qb), (g, gb))] for b in range(2)]
    own_r = [mv.here(s.at[pl.ds(2 * m, 2)], res.at[kv, :, :, pl.ds(mine_r + m * T2, T2)]) for kv, s in enumerate((rk, rv))]
    own_p = [mv.here(pk.at[0], pk0.at[:, zl, pl.ds(y * 256, 256)]), mv.here(pv.at[0], pv0.at[:, zl, pl.ds(y * 256, 256)]),
             mv.here(pk.at[1], pre1.at[0, :, zl, pl.ds(y * 256, 256)]), mv.here(pv.at[1], pre1.at[1, :, zl, pl.ds(y * 256, 256)])]
    peers = [mate, cross] + zy + [zx[k] for k in (4, 5, 6)] + xc
    barrier = pltpu.get_barrier_semaphore()
    for peer in peers:
        pl.semaphore_signal(barrier, inc=1, device_id=peer, device_id_type=MESH)
    pl.semaphore_wait(barrier, len(peers))

    pk_at = lambda z, yy: pk0.at[:, z, pl.ds(yy * 256 + half, 128)]
    pv_at = lambda z, yy: pv0.at[:, z, pl.ds(yy * 256 + half, 128)]
    p1_at = lambda z, yy: pre1.at[:, :, z, pl.ds(yy * 256 + half, 128)]
    r_at = (lambda xx: res.at[:, 0, 0, pl.ds(xx * 256 + half, 128)], lambda xx: res.at[:, 1, 0, pl.ds(xx * 256 + half, 128)],
            lambda xx: res.at[:, :, 1, pl.ds(xx * 256 + half, 128)])

    def swap_in(b, s, d):
        return mv.to(s.at[b, :, pl.ds(16 * (1 - m), 16)], d.at[b, pl.ds(T2 * m, T2)], mate)

    def swap_r(b):
        return [mv.to(s.at[pl.ds(2 * (1 - m), 2), b], res.at[kv, :, b, pl.ds(mine_r + m * T2, T2)], mate) for kv, s in enumerate((rk, rv))]

    def spread_y(src, at):
        return [mv.to(src, at(zl, y), w) for w in ys]

    def pass_z(cp, at):
        got(cp if isinstance(cp, list) else [cp])
        return [mv.to(at(1 - zl, y), at(1 - zl, y), w) for w in ys], [mv.to(at(1 - zl, y), at(1 - zl, y), sib)]

    def pass_y(z, cps, at):
        sent = []
        for d in (0, 2, 1):
            yy = (y + 3 - d) % 4
            got(cps[d] if isinstance(cps[d], list) else [cps[d]])
            sent.append(mv.to(at(z, yy), at(z, yy), sib))
        return sent

    def spread_r(u):
        at = r_at[u](x)
        return [mv.to(at, at, w) for w in xs], [mv.to(at, at, sib)]

    def pass_r(u, cps):
        sent = []
        for d in (0, 2, 1):
            cps[d].wait_recv()
            at = r_at[u]((x + 3 - d) % 4)
            sent.append(mv.to(at, at, sib))
        return sent

    mine_k, mine_v = pk.at[0, :, pl.ds(half, 128)], pv.at[0, :, pl.ds(half, 128)]
    mine_1 = pk.at[1, :, pl.ds(half, 128)], pv.at[1, :, pl.ds(half, 128)]
    p1_of = lambda kv: pre1.at[kv, :, zl, pl.ds(y * 256 + half, 128)]
    kz = mv.to(mine_k, pk_at(zl, y), zmate)
    ky = spread_y(mine_k, pk_at)
    vz = mv.to(mine_v, pv_at(zl, y), zmate)
    rz0 = swap_r(0)
    q_in = [swap_in(0, q, qb), None]
    pz = [mv.to(mine_1[kv], p1_of(kv), zmate) for kv in range(2)]
    g_in = [swap_in(0, g, gb), None]
    rz1 = swap_r(1)
    q_in[1], g_in[1] = swap_in(1, q, qb), swap_in(1, g, gb)
    ky2, ks = pass_z(kz, pk_at)
    vy = spread_y(mine_v, pv_at)
    vy2, vs = pass_z(vz, pv_at)
    for cp in own_r:
        cp.wait()
    got(rz0)
    rx0, rs0 = spread_r(0)
    rx1, rs1 = spread_r(1)
    py = [[mv.to(mine_1[kv], p1_of(kv), w) for kv in range(2)] for w in ys]
    ks += pass_y(zl, ky, pk_at)
    ks += pass_y(1 - zl, ky2, pk_at)
    for cp in own_q[0] + own_p:
        cp.wait()
    got([q_in[0]] + ks)

    def prefix_rows(h, kv, prompt, i):
        if h == 0:
            ref = pk0 if kv == 0 else pv0
            return ref[prompt, i]
        return pre1[kv, prompt, i]

    def limits(b, rc, resp):
        if not resp:
            return plen_ref[pid[2 * p + b]] - 1
        t = pos0 + rc // G + lax.broadcasted_iota(jnp.int32, (RC, 1), 0) // G
        return jnp.minimum(t, rlen_ref[2 * p + b] - 1)

    def head_rows(ref, b, h, rc):
        a = ref[b, pl.ds(rc // G, RC // G)].astype(F32)
        return a[:, h * G : (h + 1) * G].reshape(RC, HD)

    def pass_a(h, b, before_resp=None):
        prompt = pid[2 * p + b]
        for rc in range(0, R, RC):
            rows = pl.ds(rc, RC)
            a = head_rows(qb, b, h, rc)
            qr[rows] = a.astype(BF)
            a = a * C2
            hi = a.astype(BF)
            qhl[rows, 0:HD] = hi
            qhl[rows, HD : 2 * HD] = (a - hi.astype(F32)).astype(BF)
        mx[...] = jnp.full_like(mx, -jnp.inf)

        def block(kb, col0, base, resp):
            kk = jnp.concatenate([kb, kb], axis=1)
            col = base + lax.broadcasted_iota(jnp.int32, (RC, KB), 1)
            for rc in range(0, R, RC):
                rows = pl.ds(rc, RC)
                s = dot(qhl[rows], kk, NT)
                s = jnp.where(col <= limits(b, rc, resp), s, -1e30)
                S[rows, pl.ds(col0, KB)] = s
                top = mx[rows]
                for k in range(0, KB, 128):
                    top = jnp.maximum(top, s[:, k : k + 128])
                mx[rows] = top

        def step(i, _):
            start = pl.multiple_of(i * KB, KB)
            block(prefix_rows(h, 0, prompt, i), start, start, False)
            return 0

        lax.fori_loop(0, PRE // KB, step, 0)
        if before_resp is not None:
            before_resp()
        block(res[0, h, b], PRE, 0, True)
        for rc in range(0, R, RC):
            rows = pl.ds(rc, RC)
            mx[rows] = jnp.broadcast_to(jnp.max(mx[rows], axis=1, keepdims=True), (RC, 128))

    def pass_b(h, b, before_end=None):
        prompt = pid[2 * p + b]
        ls[...] = jnp.zeros_like(ls)
        oacc[...] = jnp.zeros_like(oacc)

        def block(vb, col0):
            cols = pl.ds(col0, KB)
            for rc in range(0, R, RC):
                rows = pl.ds(rc, RC)
                top = mx[rows]
                s = S[rows, cols]
                total = ls[rows]
                parts = []
                for k in range(0, KB, 128):
                    e = jnp.exp2(s[:, k : k + 128] - top)
                    total = total + e
                    parts.append(e.astype(BF))
                ls[rows] = total
                pb = jnp.concatenate(parts, axis=1)
                Pm[rows, cols] = pb
                oacc[rows] += dot(pb, vb, NN)

        def step(i, _):
            block(prefix_rows(h, 1, prompt, i), pl.multiple_of(i * KB, KB))
            return 0

        lax.fori_loop(0, PRE // KB, step, 0)
        block(res[1, h, b], PRE)
        if before_end is not None:
            before_end()
        for rc in range(0, R, RC):
            rows = pl.ds(rc, RC)
            il = 1.0 / jnp.sum(ls[rows], axis=1, keepdims=True)
            o = (oacc[rows] * il).astype(BF).astype(F32)
            if h == 0:
                oh[b, rows] = o
            else:
                both = jnp.concatenate([oh[b, rows].reshape(RC // G, G, HD), o.reshape(RC // G, G, HD)], axis=1)
                ob[b, pl.ds(rc // G, RC // G)] = both.astype(BF)
            d = head_rows(gb, b, h, rc)
            t = pos0 + rc // G + lax.broadcasted_iota(jnp.int32, (RC, 1), 0) // G
            d = jnp.where(t < rlen_ref[2 * p + b], d, 0.0)
            delta = jnp.sum(d * o, axis=1, keepdims=True)
            dr[rows] = (d * il).astype(BF)
            mx[rows] = jnp.broadcast_to(delta * il, (RC, 128))

    def pass_c(h, b, hooks=()):
        prompt = pid[2 * p + b]
        if not hooks:
            dqacc[...] = jnp.zeros_like(dqacc)

        def block(kb, vb, col0):
            cols = pl.ds(col0, KB)
            dv = dot(dr[...], Pm[:, cols], TN).T
            for rc in range(0, R, RC):
                rows = pl.ds(rc, RC)
                dp = dot(dr[rows], vb, NT)
                e = Pm[rows, cols].astype(F32)
                dl = mx[rows]
                ds = jnp.concatenate([e[:, k : k + 128] * (dp[:, k : k + 128] - dl) for k in range(0, KB, 128)], axis=1).astype(BF)
                Pm[rows, cols] = ds
                if not hooks:
                    dqacc[rows] += dot(ds, kb, NN)
            dk = dot(qr[...], Pm[:, cols], TN).T * INV
            return dk, dv

        def step(i, _):
            dkv = block(prefix_rows(h, 0, prompt, i), prefix_rows(h, 1, prompt, i), i * KB if isinstance(i, int) else pl.multiple_of(i * KB, KB))
            for kv in range(2):
                if b == 0:
                    X[h, kv, i] = dkv[kv]
                else:
                    before = pid[2 * p]
                    for a in range(2):
                        e = jnp.where(before == a, X[h, kv, i], 0.0) + jnp.where(prompt == a, dkv[kv], 0.0)
                        tm[h, kv, a, i] = e.astype(BF).reshape(4, 4, 64, HD)
            return 0

        if hooks:
            for i in range(PRE // KB):
                step(i, 0)
                hooks[i]()
        else:
            lax.fori_loop(0, PRE // KB, step, 0)
        dkv = block(res[0, h, b], res[1, h, b], PRE)
        for kv in range(2):
            tm[h, kv, 2, b] = dkv[kv].astype(BF).reshape(4, 4, 64, HD)
        if hooks:
            hooks[2]()
            for rc in range(0, R, RC):
                rows = pl.ds(rc, RC)
                t = dot(Pm[rows, PRE:], res[0, h, b], NN)
                for i in range(PRE // KB):
                    t = t + dot(Pm[rows, pl.ds(i * KB, KB)], prefix_rows(h, 0, prompt, i), NN)
                dqacc[rows] = t
        for rc in range(0, R, RC):
            rows = pl.ds(rc, RC)
            e = dqacc[rows] * INV
            if h == 0:
                dqh[b, rows] = e
            else:
                both = jnp.concatenate([dqh[b, rows].reshape(RC // G, G, HD), e.reshape(RC // G, G, HD)], axis=1)
                dqb[b, pl.ds(rc // G, RC // G)] = both.astype(BF)

    ends = []

    def swap_out(b, s, d):
        ends.append(mv.to(s.at[b, pl.ds(T2 * (1 - m), T2)], d.at[b, :, pl.ds(16 * m, 16)], mate))
        owns.append(mv.here(s.at[b, pl.ds(T2 * m, T2)], d.at[b, :, pl.ds(16 * m, 16)]))

    owns = []

    def trade(h, u):
        return mv.to(tm.at[h, 1 - c, 0:2, u], far.at[h, 0:2, u], sib)

    def pair_sum(h, u, cp):
        cp.wait_recv()
        for i in range(2):
            for k in range(4):
                s0[h, i, u, k] = (tm[h, c, i, u, k].astype(F32) + far[h, i, u, k].astype(F32)).astype(BF)
        return ([mv.to(s0.at[h, 0, u, :, (x + 1 + d) % 4], r1.at[h, 0, d, u], xs[d]) for d in range(3)],
                [mv.to(s0.at[h, 1, u, (y + 1 + d) % 4], r1.at[h, 1, d, u], ys[d]) for d in range(3)])

    def second(h, cps):
        sent = []
        for a in range(2):
            for j in range(2):
                got(cps[j][a])
                for k in range(4):
                    t = (s0[h, 0, j, k, x] if a == 0 else s0[h, 1, j, y, k]).astype(F32)
                    for d in range(3):
                        t = t + r1[h, a, d, j, k].astype(F32)
                    s1[h, a, j, k] = t.astype(BF)
            at = y if a == 0 else x
            for n in range(1, 8):
                sent.append(mv.to(s1.at[h, a, (zl + n // 4) % 2, (at + n % 4) % 4], r2.at[h, a, n - 1], (zy if a == 0 else zx)[n - 1]))
        return sent

    def final(h, cps):
        got(cps)
        for a in range(2):
            t = s1[h, a, zl, y if a == 0 else x].astype(F32)
            for n in range(7):
                t = t + r2[h, a, n].astype(F32)
            fin[c, h, a, x] = t.astype(BF)
        at = fin.at[c, h, :, x]
        ends.extend([mv.to(at, at, w) for w in xc])

    def trade_r(h, b):
        return mv.to(tm.at[h, 1 - c, 2, b], far.at[h, 2, b], sib)

    def pair_sum_r(h, b, cp):
        cp.wait_recv()
        for k in range(4):
            s0[h, 2, b, k] = (tm[h, c, 2, b, k].astype(F32) + far[h, 2, b, k].astype(F32)).astype(BF)
        return [mv.to(s0.at[h, 2, b, (x + 1 + d) % 4], rr1.at[h, d, b], xs[d]) for d in range(3)]

    def final_r(h, b, cps):
        got(cps)
        for k in range(4):
            t = s0[h, 2, b, x, k].astype(F32)
            for d in range(3):
                t = t + rr1[h, d, b, k].astype(F32)
            rs[h, b, k] = t.astype(BF)
        at = fr.at[c, 2 * m + h, b]
        owns.append(mv.here(rs.at[h, b, 2 * c + m], at))
        for core, part, w in ((1 - c, m, sib), (c, 1 - m, mate), (1 - c, 1 - m, cross)):
            ends.append(mv.to(rs.at[h, b, 2 * core + part], at, w))

    later = {}

    def resp_here():
        later["y"] = pass_z(pz, p1_at)
        vs.extend(pass_y(zl, vy, pv_at))
        got(rs0 + pass_r(0, rx0))

    pass_a(0, 0, resp_here)
    py2, ps = later["y"]
    vs += pass_y(1 - zl, vy2, pv_at)
    rs1 += pass_r(1, rx1)
    got(vs)
    pass_b(0, 0, lambda: got([g_in[0]]))
    ps += pass_y(zl, py, p1_at)
    got(rz1)
    rx2, rs2 = spread_r(2)
    pass_c(0, 0)
    t00 = trade_r(0, 0)
    ps += pass_y(1 - zl, py2, p1_at)
    got(ps + rs1)
    pass_a(1, 0)
    t00 = pair_sum_r(0, 0, t00)
    rs2 += pass_r(2, rx2)
    pass_b(1, 0)
    swap_out(0, ob, out)
    pass_c(1, 0)
    t10 = trade_r(1, 0)
    swap_out(0, dqb, dout)
    final_r(0, 0, t00)
    for cp in own_q[1]:
        cp.wait()
    got(q_in[1:] + g_in[1:] + rs2)
    pass_a(0, 1)
    t10 = pair_sum_r(1, 0, t10)
    pass_b(0, 1)
    pass_c(0, 1)
    a0 = [trade(0, 0), trade(0, 1)]
    t01 = trade_r(0, 1)
    final_r(1, 0, t10)
    pass_a(1, 1)
    a0 = [pair_sum(0, u, a0[u]) for u in range(2)]
    t01 = pair_sum_r(0, 1, t01)
    pass_b(1, 1)
    swap_out(1, ob, out)
    b0 = second(0, a0)
    t11, a1 = [None], [None, None]

    def after_first():
        a1[0] = trade(1, 0)
        final_r(0, 1, t01)

    def after_second():
        a1[1] = trade(1, 1)
        a1[0] = pair_sum(1, 0, a1[0])

    def after_resp():
        t11[0] = trade_r(1, 1)
        a1[1] = pair_sum(1, 1, a1[1])

    pass_c(1, 1, (after_first, after_second, after_resp))
    swap_out(1, dqb, dout)
    t11 = pair_sum_r(1, 1, t11[0])
    final(0, b0)
    b1 = second(1, a1)
    final_r(1, 1, t11)
    final(1, b1)
    got(ends)
    for cp in owns:
        cp.wait()
    for cp in [mv.here(fin.at[0], fin_k), mv.here(fin.at[1], fin_v), mv.here(fr.at[0], fr_k), mv.here(fr.at[1], fr_v)]:
        cp.wait()
    mv.drain()


def fused(pid, plens, rlens, q, g, rk, rv, pk, pv):
    v = pltpu.VMEM
    n = 200
    return pl.pallas_call(
        kernel,
        out_shape=[jax.ShapeDtypeStruct((2, T2, 32, HD), BF)] * 2
        + [jax.ShapeDtypeStruct((2, 2, 4, 64, HD), BF)] * 2 + [jax.ShapeDtypeStruct((4, 2, 64, HD), BF)] * 2,
        in_specs=[SM] * 3 + [HBM] * 6,
        out_specs=[HBM] * 6,
        scratch_shapes=[
            v((2, T, 16, HD), BF), v((2, T, 16, HD), BF),
            v((2, 2, 1024, HD), BF), v((2, 2, 1024, HD), BF), v((2, 2, 2, 1024, HD), BF), v((2, 2, 2, 1024, HD), BF),
            v((R, PRE + RL), F32), v((R, PRE + RL), BF),
            v((R, 2 * HD), BF), v((R, HD), BF), v((R, HD), BF),
            v((R, 128), F32), v((R, 128), F32), v((R, HD), F32), v((R, HD), F32),
            v((2, 2, 2, 1024, HD), F32), v((2, R, HD), F32), v((2, R, HD), F32), v((2, T, 16, HD), BF), v((2, T, 16, HD), BF),
            v((2, 2, 3, 2, 4, 4, 64, HD), BF), v((2, 3, 2, 4, 4, 64, HD), BF), v((2, 3, 2, 4, 4, 64, HD), BF),
            v((2, 2, 3, 2, 4, 64, HD), BF), v((2, 2, 2, 4, 64, HD), BF),
            v((2, 2, 7, 64, HD), BF), v((2, 3, 2, 4, 64, HD), BF), v((2, 2, 4, 64, HD), BF),
            v((2, 2, 2, 4, 64, HD), BF), v((2, 4, 2, 64, HD), BF),
            pltpu.SemaphoreType.DMA((n,)), pltpu.SemaphoreType.DMA((n,)), pltpu.SemaphoreType.DMA((32,)),
        ],
        compiler_params=pltpu.CompilerParams(collective_id=1, has_side_effects=True, vmem_limit_bytes=62 * 2**20),
    )(pid, plens, rlens, q, g, rk, rv, pk, pv)


def per_device(queries, resp_keys, resp_values, prefix_keys, prefix_values, grad_out, prompt_ids, prefix_lengths, resp_lengths):
    rk, rv = (a.transpose(2, 0, 1, 3) for a in (resp_keys, resp_values))
    pk, pv = (a.transpose(2, 0, 1, 3) for a in (prefix_keys, prefix_values))
    attention, d_queries, fin_k, fin_v, fr_k, fr_v = fused(prompt_ids, prefix_lengths, resp_lengths, queries, grad_out, rk, rv, pk, pv)
    fins = [a.reshape(2, 2, 256, HD).transpose(1, 2, 0, 3) for a in (fin_k, fin_v)]
    frs = [a.transpose(1, 2, 0, 3) for a in (fr_k, fr_v)]
    return (attention, d_queries, *frs, *fins)


def solution(mesh):
    rows = P("prefix", ("resp", "mp"), None, None)
    pre = P(None, "prefix", "mp", None)
    return jax.shard_map(
        per_device,
        mesh=mesh,
        in_specs=(rows, rows, rows, pre, pre, rows, P(), P(), P()),
        out_specs=(rows, rows, rows, rows, pre, pre),
        check_vma=False,
    )
```

```python
import math

import jax
import jax.numpy as jnp
from jax import lax
from jax.experimental import pallas as pl
from jax.experimental.pallas import tpu as pltpu
from jax.sharding import PartitionSpec as P

HD = 128
PRE = 2048
RL = 1024
T = 128
T2 = T // 2
G = 8
R = T * G
KB = 1024
RC = 256
UN = 2
NT = (((1,), (1,)), ((), ()))
NN = (((1,), (0,)), ((), ()))
TN = (((0,), (0,)), ((), ()))
MESH = pl.DeviceIdType.MESH
HBM = pl.BlockSpec(memory_space=pl.ANY)
VM = pl.BlockSpec(memory_space=pltpu.VMEM)
SM = pl.BlockSpec(memory_space=pltpu.SMEM)
BF = jnp.bfloat16
F32 = jnp.float32
INV = 1.0 / math.sqrt(HD)
C2 = math.log2(math.e) / math.sqrt(HD)


def dot(a, b, dims):
    return lax.dot_general(a, b, dims, preferred_element_type=F32)


class Mover:
    def __init__(self, send, recv, local):
        self.send, self.recv, self.local, self.n, self.m = send, recv, local, 0, 0
        self.remote = []

    def to(self, src, dst, where):
        cp = pltpu.make_async_remote_copy(
            src_ref=src, dst_ref=dst, send_sem=self.send.at[self.n], recv_sem=self.recv.at[self.n],
            device_id=where, device_id_type=MESH)
        self.n += 1
        cp.start()
        self.remote.append(cp)
        return cp

    def here(self, src, dst):
        cp = pltpu.make_async_copy(src, dst, self.local.at[self.m])
        self.m += 1
        cp.start()
        return cp

    def drain(self):
        for cp in self.remote:
            cp.wait_send()


def got(copies):
    for cp in copies:
        cp.wait_recv()


def kernel(pid, plen_ref, rlen_ref, q, g, rk_in, rv_in, pk_in, pv_in, out, dout, fin, fr,
           qb, gb, pk0, pv0, pre1, res, S, Pm, qhl, qr, dr, mx, ls, oacc, dqacc, X, oh, dqh, ob, dqb,
           tm, far, s0, r1, s1, r2, rr1, rs, rkt, pkt, send, recv, local):
    p, r, m = lax.axis_index("prefix"), lax.axis_index("resp"), lax.axis_index("mp")
    zl, y, x, c = p // 4, p % 4, r // 2, r % 2
    sib = {"resp": x * 2 + 1 - c}
    mate = {"mp": 1 - m}
    zmate = {"prefix": (1 - zl) * 4 + y}
    xs = [{"resp": ((x + d) % 4) * 2 + c} for d in (1, 2, 3)]
    ys = [{"prefix": zl * 4 + (y + d) % 4} for d in (1, 2, 3)]
    cross = {"resp": x * 2 + 1 - c, "mp": 1 - m}
    zy = [{"prefix": ((zl + dz) % 2) * 4 + (y + d) % 4} for dz in range(2) for d in range(4)][1:]
    zx = [{"prefix": ((zl + dz) % 2) * 4 + y, "resp": ((x + d) % 4) * 2 + c} for dz in range(2) for d in range(4)][1:]
    xc = [{"resp": ((x + d) % 4) * 2 + (c + dc) % 2} for dc in range(2) for d in range(4)][1:]
    mv = Mover(send, recv, local)
    pos0 = r * T
    mine_r = r * T
    half = c * 128

    own_q = [[mv.here(s.at[b, :, pl.ds(16 * m, 16)], d.at[b, pl.ds(T2 * m, T2)]) for s, d in ((q, qb), (g, gb))] for b in range(2)]
    for kv in range(2):
        for b in range(2):
            rkt[kv, :, b] = jnp.transpose((rk_in, rv_in)[kv][b], (1, 0, 2))
            pkt[kv, :, b] = jnp.transpose((pk_in, pv_in)[kv][b], (1, 0, 2))
    rk, rv, pk, pv = rkt.at[0], rkt.at[1], pkt.at[0], pkt.at[1]
    own_r = [mv.here(s.at[pl.ds(2 * m, 2)], res.at[kv, :, :, pl.ds(mine_r + m * T2, T2)]) for kv, s in enumerate((rk, rv))]
    own_p = [mv.here(pk.at[0], pk0.at[:, zl, pl.ds(y * 256, 256)]), mv.here(pv.at[0], pv0.at[:, zl, pl.ds(y * 256, 256)]),
             mv.here(pk.at[1], pre1.at[0, :, zl, pl.ds(y * 256, 256)]), mv.here(pv.at[1], pre1.at[1, :, zl, pl.ds(y * 256, 256)])]
    peers = [mate, cross] + zy + [zx[k] for k in (4, 5, 6)] + xc
    barrier = pltpu.get_barrier_semaphore()
    for peer in peers:
        pl.semaphore_signal(barrier, inc=1, device_id=peer, device_id_type=MESH)
    pl.semaphore_wait(barrier, len(peers))

    pk_at = lambda z, yy: pk0.at[:, z, pl.ds(yy * 256 + half, 128)]
    pv_at = lambda z, yy: pv0.at[:, z, pl.ds(yy * 256 + half, 128)]
    p1_at = lambda z, yy: pre1.at[:, :, z, pl.ds(yy * 256 + half, 128)]
    r_at = (lambda xx: res.at[:, 0, 0, pl.ds(xx * 256 + half, 128)], lambda xx: res.at[:, 1, 0, pl.ds(xx * 256 + half, 128)],
            lambda xx: res.at[:, :, 1, pl.ds(xx * 256 + half, 128)])

    def swap_in(b, s, d):
        return mv.to(s.at[b, :, pl.ds(16 * (1 - m), 16)], d.at[b, pl.ds(T2 * m, T2)], mate)

    def swap_r(b):
        return [mv.to(s.at[pl.ds(2 * (1 - m), 2), b], res.at[kv, :, b, pl.ds(mine_r + m * T2, T2)], mate) for kv, s in enumerate((rk, rv))]

    def spread_y(src, at):
        return [mv.to(src, at(zl, y), w) for w in ys]

    def pass_z(cp, at):
        got(cp if isinstance(cp, list) else [cp])
        return [mv.to(at(1 - zl, y), at(1 - zl, y), w) for w in ys], [mv.to(at(1 - zl, y), at(1 - zl, y), sib)]

    def pass_y(z, cps, at):
        sent = []
        for d in (0, 2, 1):
            yy = (y + 3 - d) % 4
            got(cps[d] if isinstance(cps[d], list) else [cps[d]])
            sent.append(mv.to(at(z, yy), at(z, yy), sib))
        return sent

    def spread_r(u):
        at = r_at[u](x)
        return [mv.to(at, at, w) for w in xs], [mv.to(at, at, sib)]

    def pass_r(u, cps):
        sent = []
        for d in (0, 2, 1):
            cps[d].wait_recv()
            at = r_at[u]((x + 3 - d) % 4)
            sent.append(mv.to(at, at, sib))
        return sent

    mine_k, mine_v = pk.at[0, :, pl.ds(half, 128)], pv.at[0, :, pl.ds(half, 128)]
    mine_1 = pk.at[1, :, pl.ds(half, 128)], pv.at[1, :, pl.ds(half, 128)]
    p1_of = lambda kv: pre1.at[kv, :, zl, pl.ds(y * 256 + half, 128)]
    kz = mv.to(mine_k, pk_at(zl, y), zmate)
    ky = spread_y(mine_k, pk_at)
    vz = mv.to(mine_v, pv_at(zl, y), zmate)
    rz0 = swap_r(0)
    q_in = [swap_in(0, q, qb), None]
    pz = [mv.to(mine_1[kv], p1_of(kv), zmate) for kv in range(2)]
    g_in = [swap_in(0, g, gb), None]
    rz1 = swap_r(1)
    q_in[1], g_in[1] = swap_in(1, q, qb), swap_in(1, g, gb)
    ky2, ks = pass_z(kz, pk_at)
    vy = spread_y(mine_v, pv_at)
    vy2, vs = pass_z(vz, pv_at)
    for cp in own_r:
        cp.wait()
    got(rz0)
    rx0, rs0 = spread_r(0)
    rx1, rs1 = spread_r(1)
    py = [[mv.to(mine_1[kv], p1_of(kv), w) for kv in range(2)] for w in ys]
    ks += pass_y(zl, ky, pk_at)
    ks += pass_y(1 - zl, ky2, pk_at)
    for cp in own_q[0] + own_p:
        cp.wait()
    got([q_in[0]] + ks)

    def prefix_rows(h, kv, prompt, i):
        if h == 0:
            ref = pk0 if kv == 0 else pv0
            return ref[prompt, i]
        return pre1[kv, prompt, i]

    def limits(b, rc, resp):
        if not resp:
            return plen_ref[pid[2 * p + b]] - 1
        t = pos0 + rc // G + lax.broadcasted_iota(jnp.int32, (RC, 1), 0) // G
        return jnp.minimum(t, rlen_ref[2 * p + b] - 1)

    def head_rows(ref, b, h, rc):
        a = ref[b, pl.ds(rc // G, RC // G)].astype(F32)
        return a[:, h * G : (h + 1) * G].reshape(RC, HD)

    def pass_a(h, b, before_resp=None):
        prompt = pid[2 * p + b]
        for rc in range(0, R, RC):
            rows = pl.ds(rc, RC)
            a = head_rows(qb, b, h, rc)
            qr[rows] = a.astype(BF)
            a = a * C2
            hi = a.astype(BF)
            qhl[rows, 0:HD] = hi
            qhl[rows, HD : 2 * HD] = (a - hi.astype(F32)).astype(BF)
        mx[...] = jnp.full_like(mx, -jnp.inf)

        def block(load, col0, base, resp):
            col = base + lax.broadcasted_iota(jnp.int32, (RC, KB), 1)

            def chunk(n, _):
                for u in range(UN):
                    rc = (n * UN + u) * RC
                    rows = pl.ds(pl.multiple_of(rc, RC), RC)
                    kb = load()
                    s = dot(qhl[rows], jnp.concatenate([kb, kb], axis=1), NT)
                    s = jnp.where(col <= limits(b, rc, resp), s, -1e30)
                    S[rows, pl.ds(col0, KB)] = s
                    top = mx[rows]
                    for k in range(0, KB, 128):
                        top = jnp.maximum(top, s[:, k : k + 128])
                    mx[rows] = top
                return 0

            lax.fori_loop(0, R // RC // UN, chunk, 0)

        def step(i, _):
            start = pl.multiple_of(i * KB, KB)
            block(lambda: prefix_rows(h, 0, prompt, i), start, start, False)
            return 0

        lax.fori_loop(0, PRE // KB, step, 0)
        if before_resp is not None:
            before_resp()
        block(lambda: res[0, h, b], PRE, 0, True)
        for rc in range(0, R, RC):
            rows = pl.ds(rc, RC)
            mx[rows] = jnp.broadcast_to(jnp.max(mx[rows], axis=1, keepdims=True), (RC, 128))

    def pass_b(h, b, before_end=None):
        prompt = pid[2 * p + b]
        ls[...] = jnp.zeros_like(ls)
        oacc[...] = jnp.zeros_like(oacc)

        def block(load, col0):
            cols = pl.ds(col0, KB)

            def chunk(n, _):
                for u in range(UN):
                    rows = pl.ds(pl.multiple_of((n * UN + u) * RC, RC), RC)
                    top = mx[rows]
                    s = S[rows, cols]
                    total = ls[rows]
                    parts = []
                    for k in range(0, KB, 128):
                        e = jnp.exp2(s[:, k : k + 128] - top)
                        total = total + e
                        parts.append(e.astype(BF))
                    ls[rows] = total
                    pb = jnp.concatenate(parts, axis=1)
                    Pm[rows, cols] = pb
                    oacc[rows] += dot(pb, load(), NN)
                return 0

            lax.fori_loop(0, R // RC // UN, chunk, 0)

        def step(i, _):
            block(lambda: prefix_rows(h, 1, prompt, i), pl.multiple_of(i * KB, KB))
            return 0

        lax.fori_loop(0, PRE // KB, step, 0)
        block(lambda: res[1, h, b], PRE)
        if before_end is not None:
            before_end()
        for rc in range(0, R, RC):
            rows = pl.ds(rc, RC)
            il = 1.0 / jnp.sum(ls[rows], axis=1, keepdims=True)
            o = (oacc[rows] * il).astype(BF).astype(F32)
            if h == 0:
                oh[b, rows] = o
            else:
                both = jnp.concatenate([oh[b, rows].reshape(RC // G, G, HD), o.reshape(RC // G, G, HD)], axis=1)
                ob[b, pl.ds(rc // G, RC // G)] = both.astype(BF)
            d = head_rows(gb, b, h, rc)
            t = pos0 + rc // G + lax.broadcasted_iota(jnp.int32, (RC, 1), 0) // G
            d = jnp.where(t < rlen_ref[2 * p + b], d, 0.0)
            delta = jnp.sum(d * o, axis=1, keepdims=True)
            dr[rows] = (d * il).astype(BF)
            mx[rows] = jnp.broadcast_to(delta * il, (RC, 128))

    def pass_c(h, b, hooks=()):
        prompt = pid[2 * p + b]
        if not hooks:
            dqacc[...] = jnp.zeros_like(dqacc)

        def block(load_k, load_v, col0):
            cols = pl.ds(col0, KB)
            dv = dot(dr[...], Pm[:, cols], TN).T

            def chunk(n, _):
                for u in range(UN):
                    rows = pl.ds(pl.multiple_of((n * UN + u) * RC, RC), RC)
                    dp = dot(dr[rows], load_v(), NT)
                    e = Pm[rows, cols].astype(F32)
                    dl = mx[rows]
                    ds = jnp.concatenate([e[:, k : k + 128] * (dp[:, k : k + 128] - dl) for k in range(0, KB, 128)], axis=1).astype(BF)
                    Pm[rows, cols] = ds
                    if not hooks:
                        dqacc[rows] += dot(ds, load_k(), NN)
                return 0

            lax.fori_loop(0, R // RC // UN, chunk, 0)
            dk = dot(qr[...], Pm[:, cols], TN).T * INV
            return dk, dv

        def step(i, _):
            dkv = block(lambda: prefix_rows(h, 0, prompt, i), lambda: prefix_rows(h, 1, prompt, i), i * KB if isinstance(i, int) else pl.multiple_of(i * KB, KB))
            for kv in range(2):
                if b == 0:
                    X[h, kv, i] = dkv[kv]
                else:
                    before = pid[2 * p]
                    for a in range(2):
                        e = jnp.where(before == a, X[h, kv, i], 0.0) + jnp.where(prompt == a, dkv[kv], 0.0)
                        tm[h, kv, a, i] = e.astype(BF).reshape(4, 4, 64, HD)
            return 0

        if hooks:
            for i in range(PRE // KB):
                step(i, 0)
                hooks[i]()
        else:
            lax.fori_loop(0, PRE // KB, step, 0)
        dkv = block(lambda: res[0, h, b], lambda: res[1, h, b], PRE)
        for kv in range(2):
            tm[h, kv, 2, b] = dkv[kv].astype(BF).reshape(4, 4, 64, HD)
        if hooks:
            hooks[2]()
            for rc in range(0, R, RC):
                rows = pl.ds(rc, RC)
                t = dot(Pm[rows, PRE:], res[0, h, b], NN)
                for i in range(PRE // KB):
                    t = t + dot(Pm[rows, pl.ds(i * KB, KB)], prefix_rows(h, 0, prompt, i), NN)
                dqacc[rows] = t
        for rc in range(0, R, RC):
            rows = pl.ds(rc, RC)
            e = dqacc[rows] * INV
            if h == 0:
                dqh[b, rows] = e
            else:
                both = jnp.concatenate([dqh[b, rows].reshape(RC // G, G, HD), e.reshape(RC // G, G, HD)], axis=1)
                dqb[b, pl.ds(rc // G, RC // G)] = both.astype(BF)

    ends = []

    def swap_out(b, s, d):
        ends.append(mv.to(s.at[b, pl.ds(T2 * (1 - m), T2)], d.at[b, :, pl.ds(16 * m, 16)], mate))
        owns.append(mv.here(s.at[b, pl.ds(T2 * m, T2)], d.at[b, :, pl.ds(16 * m, 16)]))

    owns = []

    def trade(h, u):
        return mv.to(tm.at[h, 1 - c, 0:2, u], far.at[h, 0:2, u], sib)

    def pair_sum(h, u, cp):
        cp.wait_recv()
        for i in range(2):
            for k in range(4):
                s0[h, i, u, k] = (tm[h, c, i, u, k].astype(F32) + far[h, i, u, k].astype(F32)).astype(BF)
        return ([mv.to(s0.at[h, 0, u, :, (x + 1 + d) % 4], r1.at[h, 0, d, u], xs[d]) for d in range(3)],
                [mv.to(s0.at[h, 1, u, (y + 1 + d) % 4], r1.at[h, 1, d, u], ys[d]) for d in range(3)])

    def second(h, cps):
        sent = []
        for a in range(2):
            for j in range(2):
                got(cps[j][a])
                for k in range(4):
                    t = (s0[h, 0, j, k, x] if a == 0 else s0[h, 1, j, y, k]).astype(F32)
                    for d in range(3):
                        t = t + r1[h, a, d, j, k].astype(F32)
                    s1[h, a, j, k] = t.astype(BF)
            at = y if a == 0 else x
            for n in range(1, 8):
                sent.append(mv.to(s1.at[h, a, (zl + n // 4) % 2, (at + n % 4) % 4], r2.at[h, a, n - 1], (zy if a == 0 else zx)[n - 1]))
        return sent

    def final(h, cps):
        got(cps)
        for a in range(2):
            t = s1[h, a, zl, y if a == 0 else x].astype(F32)
            for n in range(7):
                t = t + r2[h, a, n].astype(F32)
            fin[c, h, a, x] = t.astype(BF)
        at = fin.at[c, h, :, x]
        ends.extend([mv.to(at, at, w) for w in xc])

    def trade_r(h, b):
        return mv.to(tm.at[h, 1 - c, 2, b], far.at[h, 2, b], sib)

    def pair_sum_r(h, b, cp):
        cp.wait_recv()
        for k in range(4):
            s0[h, 2, b, k] = (tm[h, c, 2, b, k].astype(F32) + far[h, 2, b, k].astype(F32)).astype(BF)
        return [mv.to(s0.at[h, 2, b, (x + 1 + d) % 4], rr1.at[h, d, b], xs[d]) for d in range(3)]

    def final_r(h, b, cps):
        got(cps)
        for k in range(4):
            t = s0[h, 2, b, x, k].astype(F32)
            for d in range(3):
                t = t + rr1[h, d, b, k].astype(F32)
            rs[h, b, k] = t.astype(BF)
        at = fr.at[c, 2 * m + h, b]
        owns.append(mv.here(rs.at[h, b, 2 * c + m], at))
        for core, part, w in ((1 - c, m, sib), (c, 1 - m, mate), (1 - c, 1 - m, cross)):
            ends.append(mv.to(rs.at[h, b, 2 * core + part], at, w))

    later = {}

    def resp_here():
        later["y"] = pass_z(pz, p1_at)
        vs.extend(pass_y(zl, vy, pv_at))
        got(rs0 + pass_r(0, rx0))

    pass_a(0, 0, resp_here)
    py2, ps = later["y"]
    vs += pass_y(1 - zl, vy2, pv_at)
    rs1 += pass_r(1, rx1)
    got(vs)
    pass_b(0, 0, lambda: got([g_in[0]]))
    ps += pass_y(zl, py, p1_at)
    got(rz1)
    rx2, rs2 = spread_r(2)
    pass_c(0, 0)
    t00 = trade_r(0, 0)
    ps += pass_y(1 - zl, py2, p1_at)
    got(ps + rs1)
    pass_a(1, 0)
    t00 = pair_sum_r(0, 0, t00)
    rs2 += pass_r(2, rx2)
    pass_b(1, 0)
    swap_out(0, ob, out)
    pass_c(1, 0)
    t10 = trade_r(1, 0)
    swap_out(0, dqb, dout)
    final_r(0, 0, t00)
    for cp in own_q[1]:
        cp.wait()
    got(q_in[1:] + g_in[1:] + rs2)
    pass_a(0, 1)
    t10 = pair_sum_r(1, 0, t10)
    pass_b(0, 1)
    pass_c(0, 1)
    a0 = [trade(0, 0), trade(0, 1)]
    t01 = trade_r(0, 1)
    final_r(1, 0, t10)
    pass_a(1, 1)
    a0 = [pair_sum(0, u, a0[u]) for u in range(2)]
    t01 = pair_sum_r(0, 1, t01)
    pass_b(1, 1)
    swap_out(1, ob, out)
    b0 = second(0, a0)
    t11, a1 = [None], [None, None]

    def after_first():
        a1[0] = trade(1, 0)
        final_r(0, 1, t01)

    def after_second():
        a1[1] = trade(1, 1)
        a1[0] = pair_sum(1, 0, a1[0])

    def after_resp():
        t11[0] = trade_r(1, 1)
        a1[1] = pair_sum(1, 1, a1[1])

    pass_c(1, 1, (after_first, after_second, after_resp))
    swap_out(1, dqb, dout)
    t11 = pair_sum_r(1, 1, t11[0])
    final(0, b0)
    b1 = second(1, a1)
    final_r(1, 1, t11)
    final(1, b1)
    got(ends)
    for cp in owns:
        cp.wait()
    mv.drain()


def fused(pid, plens, rlens, q, g, rk, rv, pk, pv):
    v = pltpu.VMEM
    n = 200
    return pl.pallas_call(
        kernel,
        out_shape=[jax.ShapeDtypeStruct((2, T2, 32, HD), BF)] * 2
        + [jax.ShapeDtypeStruct((2, 2, 2, 4, 64, HD), BF), jax.ShapeDtypeStruct((2, 4, 2, 64, HD), BF)],
        in_specs=[SM] * 3 + [HBM] * 2 + [VM] * 4,
        out_specs=[HBM, HBM, VM, VM],
        scratch_shapes=[
            v((2, T, 16, HD), BF), v((2, T, 16, HD), BF),
            v((2, 2, 1024, HD), BF), v((2, 2, 1024, HD), BF), v((2, 2, 2, 1024, HD), BF), v((2, 2, 2, 1024, HD), BF),
            v((R, PRE + RL), F32), v((R, PRE + RL), BF),
            v((R, 2 * HD), BF), v((R, HD), BF), v((R, HD), BF),
            v((R, 128), F32), v((R, 128), F32), v((R, HD), F32), v((R, HD), F32),
            v((2, 2, 2, 1024, HD), F32), v((2, R, HD), F32), v((2, R, HD), F32), v((2, T, 16, HD), BF), v((2, T, 16, HD), BF),
            v((2, 2, 3, 2, 4, 4, 64, HD), BF), v((2, 3, 2, 4, 4, 64, HD), BF), v((2, 3, 2, 4, 4, 64, HD), BF),
            v((2, 2, 3, 2, 4, 64, HD), BF), v((2, 2, 2, 4, 64, HD), BF),
            v((2, 2, 7, 64, HD), BF), v((2, 3, 2, 4, 64, HD), BF), v((2, 2, 4, 64, HD), BF),
            v((2, 4, 2, 64, HD), BF), v((2, 2, 2, 256, HD), BF),
            pltpu.SemaphoreType.DMA((n,)), pltpu.SemaphoreType.DMA((n,)), pltpu.SemaphoreType.DMA((32,)),
        ],
        compiler_params=pltpu.CompilerParams(collective_id=1, has_side_effects=True, vmem_limit_bytes=62 * 2**20),
    )(pid, plens, rlens, q, g, rk, rv, pk, pv)


def finish_kernel(out, dout, fin, fr, out2, dout2, dpk, dpv, drk, drv, sems):
    copies = [pltpu.make_async_copy(out, out2, sems.at[0]), pltpu.make_async_copy(dout, dout2, sems.at[1])]
    for cp in copies:
        cp.start()
    for kv, (dp, dr) in enumerate(((dpk, drk), (dpv, drv))):
        for i in range(2):
            dp[i] = jnp.transpose(fin[kv, :, i], (1, 0, 2))
            dr[i] = jnp.transpose(fr[kv, :, i], (1, 0, 2))
    for cp in copies:
        cp.wait()


def finish(out, dout, fin, fr):
    rows = jax.ShapeDtypeStruct((2, T2, 32, HD), BF)
    return pl.pallas_call(
        finish_kernel,
        out_shape=[rows] * 2 + [jax.ShapeDtypeStruct((2, 256, 2, HD), BF)] * 2 + [jax.ShapeDtypeStruct((2, T2, 4, HD), BF)] * 2,
        in_specs=[HBM, HBM, VM, VM],
        out_specs=[HBM] * 2 + [VM] * 4,
        scratch_shapes=[pltpu.SemaphoreType.DMA((2,))],
        compiler_params=pltpu.CompilerParams(vmem_limit_bytes=60 * 2**20),
    )(out, dout, fin, fr)


def per_device(queries, resp_keys, resp_values, prefix_keys, prefix_values, grad_out, prompt_ids, prefix_lengths, resp_lengths):
    out, dout, fin, fr = fused(prompt_ids, prefix_lengths, resp_lengths, queries, grad_out, resp_keys, resp_values, prefix_keys, prefix_values)
    attention, d_queries, dpk, dpv, drk, drv = finish(out, dout, fin.reshape(2, 2, 2, 256, HD), fr)
    return (attention, d_queries, drk, drv, dpk, dpv)


def solution(mesh):
    rows = P("prefix", ("resp", "mp"), None, None)
    pre = P(None, "prefix", "mp", None)
    return jax.shard_map(
        per_device,
        mesh=mesh,
        in_specs=(rows, rows, rows, pre, pre, rows, P(), P(), P()),
        out_specs=(rows, rows, rows, rows, pre, pre),
        check_vma=False,
    )
```

```python
import math

import jax
import jax.numpy as jnp
from jax import lax
from jax.experimental import pallas as pl
from jax.experimental.pallas import tpu as pltpu
from jax.sharding import PartitionSpec as P

HD = 128
PRE = 2048
RL = 1024
T = 128
T2 = T // 2
G = 8
R = T * G
KB = 1024
RC = 256
NT = (((1,), (1,)), ((), ()))
NN = (((1,), (0,)), ((), ()))
TN = (((0,), (0,)), ((), ()))
MESH = pl.DeviceIdType.MESH
HBM = pl.BlockSpec(memory_space=pl.ANY)
VM = pl.BlockSpec(memory_space=pltpu.VMEM)
SM = pl.BlockSpec(memory_space=pltpu.SMEM)
BF = jnp.bfloat16
F32 = jnp.float32
INV = 1.0 / math.sqrt(HD)
C2 = math.log2(math.e) / math.sqrt(HD)


def dot(a, b, dims):
    return lax.dot_general(a, b, dims, preferred_element_type=F32)


class Mover:
    def __init__(self, send, recv, local):
        self.send, self.recv, self.local, self.n, self.m = send, recv, local, 0, 0
        self.remote = []

    def to(self, src, dst, where):
        cp = pltpu.make_async_remote_copy(
            src_ref=src, dst_ref=dst, send_sem=self.send.at[self.n], recv_sem=self.recv.at[self.n],
            device_id=where, device_id_type=MESH)
        self.n += 1
        cp.start()
        self.remote.append(cp)
        return cp

    def here(self, src, dst):
        cp = pltpu.make_async_copy(src, dst, self.local.at[self.m])
        self.m += 1
        cp.start()
        return cp

    def drain(self):
        for cp in self.remote:
            cp.wait_send()


def chunks(body):
    def step(n, _):
        body(pl.multiple_of(n * RC, RC))
        return 0

    lax.fori_loop(0, R // RC, step, 0)


def fours(body):
    def step(k, _):
        body(k)
        return 0

    lax.fori_loop(0, 4, step, 0)


def got(copies):
    for cp in copies:
        cp.wait_recv()


def kernel(pid, plen_ref, rlen_ref, q, g, rk_in, rv_in, pk_in, pv_in, out, dout, fin, fr,
           qb, gb, pk0, pv0, pre1, res, S, Pm, qhl, qr, dr, mx, ls, oacc, dqacc, X, oh, dqh, ob, dqb,
           tm, far, s0, r1, s1, r2, rr1, rs, rkt, pkt, send, recv, local):
    p, r, m = lax.axis_index("prefix"), lax.axis_index("resp"), lax.axis_index("mp")
    zl, y, x, c = p // 4, p % 4, r // 2, r % 2
    sib = {"resp": x * 2 + 1 - c}
    mate = {"mp": 1 - m}
    zmate = {"prefix": (1 - zl) * 4 + y}
    xs = [{"resp": ((x + d) % 4) * 2 + c} for d in (1, 2, 3)]
    ys = [{"prefix": zl * 4 + (y + d) % 4} for d in (1, 2, 3)]
    cross = {"resp": x * 2 + 1 - c, "mp": 1 - m}
    zy = [{"prefix": ((zl + dz) % 2) * 4 + (y + d) % 4} for dz in range(2) for d in range(4)][1:]
    zx = [{"prefix": ((zl + dz) % 2) * 4 + y, "resp": ((x + d) % 4) * 2 + c} for dz in range(2) for d in range(4)][1:]
    xc = [{"resp": ((x + d) % 4) * 2 + (c + dc) % 2} for dc in range(2) for d in range(4)][1:]
    mv = Mover(send, recv, local)
    pos0 = r * T
    mine_r = r * T
    half = c * 128

    own_q = [[mv.here(s.at[b, :, pl.ds(16 * m, 16)], d.at[b, pl.ds(T2 * m, T2)]) for s, d in ((q, qb), (g, gb))] for b in range(2)]
    for kv in range(2):
        for b in range(2):
            rkt[kv, :, b] = jnp.transpose((rk_in, rv_in)[kv][b], (1, 0, 2))
            pkt[kv, :, b] = jnp.transpose((pk_in, pv_in)[kv][b], (1, 0, 2))
    rk, rv, pk, pv = rkt.at[0], rkt.at[1], pkt.at[0], pkt.at[1]
    own_r = [mv.here(s.at[pl.ds(2 * m, 2)], res.at[kv, :, :, pl.ds(mine_r + m * T2, T2)]) for kv, s in enumerate((rk, rv))]
    own_p = [mv.here(pk.at[0], pk0.at[:, zl, pl.ds(y * 256, 256)]), mv.here(pv.at[0], pv0.at[:, zl, pl.ds(y * 256, 256)]),
             mv.here(pk.at[1], pre1.at[0, :, zl, pl.ds(y * 256, 256)]), mv.here(pv.at[1], pre1.at[1, :, zl, pl.ds(y * 256, 256)])]
    peers = [mate, cross] + zy + [zx[k] for k in (4, 5, 6)] + xc
    barrier = pltpu.get_barrier_semaphore()
    for peer in peers:
        pl.semaphore_signal(barrier, inc=1, device_id=peer, device_id_type=MESH)
    pl.semaphore_wait(barrier, len(peers))

    pk_at = lambda z, yy: pk0.at[:, z, pl.ds(yy * 256 + half, 128)]
    pv_at = lambda z, yy: pv0.at[:, z, pl.ds(yy * 256 + half, 128)]
    p1_at = lambda z, yy: pre1.at[:, :, z, pl.ds(yy * 256 + half, 128)]
    r_at = (lambda xx: res.at[:, 0, 0, pl.ds(xx * 256 + half, 128)], lambda xx: res.at[:, 1, 0, pl.ds(xx * 256 + half, 128)],
            lambda xx: res.at[:, :, 1, pl.ds(xx * 256 + half, 128)])

    def swap_in(b, s, d):
        return mv.to(s.at[b, :, pl.ds(16 * (1 - m), 16)], d.at[b, pl.ds(T2 * m, T2)], mate)

    def swap_r(b):
        return [mv.to(s.at[pl.ds(2 * (1 - m), 2), b], res.at[kv, :, b, pl.ds(mine_r + m * T2, T2)], mate) for kv, s in enumerate((rk, rv))]

    def spread_y(src, at):
        return [mv.to(src, at(zl, y), w) for w in ys]

    def pass_z(cp, at):
        got(cp if isinstance(cp, list) else [cp])
        return [mv.to(at(1 - zl, y), at(1 - zl, y), w) for w in ys], [mv.to(at(1 - zl, y), at(1 - zl, y), sib)]

    def pass_y(z, cps, at):
        sent = []
        for d in (0, 2, 1):
            yy = (y + 3 - d) % 4
            got(cps[d] if isinstance(cps[d], list) else [cps[d]])
            sent.append(mv.to(at(z, yy), at(z, yy), sib))
        return sent

    def spread_r(u):
        at = r_at[u](x)
        return [mv.to(at, at, w) for w in xs], [mv.to(at, at, sib)]

    def pass_r(u, cps):
        sent = []
        for d in (0, 2, 1):
            cps[d].wait_recv()
            at = r_at[u]((x + 3 - d) % 4)
            sent.append(mv.to(at, at, sib))
        return sent

    mine_k, mine_v = pk.at[0, :, pl.ds(half, 128)], pv.at[0, :, pl.ds(half, 128)]
    mine_1 = pk.at[1, :, pl.ds(half, 128)], pv.at[1, :, pl.ds(half, 128)]
    p1_of = lambda kv: pre1.at[kv, :, zl, pl.ds(y * 256 + half, 128)]
    kz = mv.to(mine_k, pk_at(zl, y), zmate)
    ky = spread_y(mine_k, pk_at)
    vz = mv.to(mine_v, pv_at(zl, y), zmate)
    rz0 = swap_r(0)
    q_in = [swap_in(0, q, qb), None]
    pz = [mv.to(mine_1[kv], p1_of(kv), zmate) for kv in range(2)]
    g_in = [swap_in(0, g, gb), None]
    rz1 = swap_r(1)
    q_in[1], g_in[1] = swap_in(1, q, qb), swap_in(1, g, gb)
    ky2, ks = pass_z(kz, pk_at)
    vy = spread_y(mine_v, pv_at)
    vy2, vs = pass_z(vz, pv_at)
    for cp in own_r:
        cp.wait()
    got(rz0)
    rx0, rs0 = spread_r(0)
    rx1, rs1 = spread_r(1)
    py = [[mv.to(mine_1[kv], p1_of(kv), w) for kv in range(2)] for w in ys]
    ks += pass_y(zl, ky, pk_at)
    ks += pass_y(1 - zl, ky2, pk_at)
    for cp in own_q[0] + own_p:
        cp.wait()
    got([q_in[0]] + ks)

    def prefix_rows(h, kv, prompt, i):
        if h == 0:
            ref = pk0 if kv == 0 else pv0
            return ref[prompt, i]
        return pre1[kv, prompt, i]

    def limits(b, rc, resp):
        if not resp:
            return plen_ref[pid[2 * p + b]] - 1
        t = pos0 + rc // G + lax.broadcasted_iota(jnp.int32, (RC, 1), 0) // G
        return jnp.minimum(t, rlen_ref[2 * p + b] - 1)

    def head_rows(ref, b, h, rc):
        a = ref[b, pl.ds(pl.multiple_of(rc // G, RC // G), RC // G)].astype(F32)
        return a[:, h * G : (h + 1) * G].reshape(RC, HD)

    def pass_a(h, b, before_resp=None):
        prompt = pid[2 * p + b]
        @chunks
        def _(rc):
            rows = pl.ds(rc, RC)
            a = head_rows(qb, b, h, rc)
            qr[rows] = a.astype(BF)
            a = a * C2
            hi = a.astype(BF)
            qhl[rows, 0:HD] = hi
            qhl[rows, HD : 2 * HD] = (a - hi.astype(F32)).astype(BF)
        mx[...] = jnp.full_like(mx, -jnp.inf)

        def block(load, col0, base, resp):
            col = base + lax.broadcasted_iota(jnp.int32, (RC, KB), 1)

            kb = load()
            kk = jnp.concatenate([kb, kb], axis=1)
            for rc in range(0, R, RC):
                rows = pl.ds(rc, RC)
                s = dot(qhl[rows], kk, NT)
                s = jnp.where(col <= limits(b, rc, resp), s, -1e30)
                S[rows, pl.ds(col0, KB)] = s
                top = mx[rows]
                for k in range(0, KB, 128):
                    top = jnp.maximum(top, s[:, k : k + 128])
                mx[rows] = top

        def step(i, _):
            start = pl.multiple_of(i * KB, KB)
            block(lambda: prefix_rows(h, 0, prompt, i), start, start, False)
            return 0

        lax.fori_loop(0, PRE // KB, step, 0)
        if before_resp is not None:
            before_resp()
        block(lambda: res[0, h, b], PRE, 0, True)
        @chunks
        def _(rc):
            rows = pl.ds(rc, RC)
            mx[rows] = jnp.broadcast_to(jnp.max(mx[rows], axis=1, keepdims=True), (RC, 128))

    def pass_b(h, b, before_end=None):
        prompt = pid[2 * p + b]
        ls[...] = jnp.zeros_like(ls)
        oacc[...] = jnp.zeros_like(oacc)

        def block(load, col0):
            cols = pl.ds(col0, KB)

            vb = load()
            for rc in range(0, R, RC):
                rows = pl.ds(rc, RC)
                top = mx[rows]
                s = S[rows, cols]
                total = ls[rows]
                parts = []
                for k in range(0, KB, 128):
                    e = jnp.exp2(s[:, k : k + 128] - top)
                    total = total + e
                    parts.append(e.astype(BF))
                ls[rows] = total
                pb = jnp.concatenate(parts, axis=1)
                Pm[rows, cols] = pb
                oacc[rows] += dot(pb, vb, NN)

        def step(i, _):
            block(lambda: prefix_rows(h, 1, prompt, i), pl.multiple_of(i * KB, KB))
            return 0

        lax.fori_loop(0, PRE // KB, step, 0)
        block(lambda: res[1, h, b], PRE)
        if before_end is not None:
            before_end()
        @chunks
        def _(rc):
            rows = pl.ds(rc, RC)
            il = 1.0 / jnp.sum(ls[rows], axis=1, keepdims=True)
            o = (oacc[rows] * il).astype(BF).astype(F32)
            if h == 0:
                oh[b, rows] = o
            else:
                both = jnp.concatenate([oh[b, rows].reshape(RC // G, G, HD), o.reshape(RC // G, G, HD)], axis=1)
                ob[b, pl.ds(pl.multiple_of(rc // G, RC // G), RC // G)] = both.astype(BF)
            d = head_rows(gb, b, h, rc)
            t = pos0 + rc // G + lax.broadcasted_iota(jnp.int32, (RC, 1), 0) // G
            d = jnp.where(t < rlen_ref[2 * p + b], d, 0.0)
            delta = jnp.sum(d * o, axis=1, keepdims=True)
            dr[rows] = (d * il).astype(BF)
            mx[rows] = jnp.broadcast_to(delta * il, (RC, 128))

    def pass_c(h, b, hooks=()):
        prompt = pid[2 * p + b]
        if not hooks:
            dqacc[...] = jnp.zeros_like(dqacc)

        def block(load_k, load_v, col0):
            cols = pl.ds(col0, KB)
            dv = dot(dr[...], Pm[:, cols], TN).T

            vb, kb = load_v(), load_k()
            for rc in range(0, R, RC):
                rows = pl.ds(rc, RC)
                dp = dot(dr[rows], vb, NT)
                e = Pm[rows, cols].astype(F32)
                dl = mx[rows]
                ds = jnp.concatenate([e[:, k : k + 128] * (dp[:, k : k + 128] - dl) for k in range(0, KB, 128)], axis=1).astype(BF)
                Pm[rows, cols] = ds
                if not hooks:
                    dqacc[rows] += dot(ds, kb, NN)
            dk = dot(qr[...], Pm[:, cols], TN).T * INV
            return dk, dv

        def step(i, _):
            dkv = block(lambda: prefix_rows(h, 0, prompt, i), lambda: prefix_rows(h, 1, prompt, i), i * KB if isinstance(i, int) else pl.multiple_of(i * KB, KB))
            for kv in range(2):
                if b == 0:
                    X[h, kv, i] = dkv[kv]
                else:
                    before = pid[2 * p]
                    for a in range(2):
                        e = jnp.where(before == a, X[h, kv, i], 0.0) + jnp.where(prompt == a, dkv[kv], 0.0)
                        tm[h, kv, a, i] = e.astype(BF).reshape(4, 4, 64, HD)
            return 0

        if hooks:
            for i in range(PRE // KB):
                step(i, 0)
                hooks[i]()
        else:
            lax.fori_loop(0, PRE // KB, step, 0)
        dkv = block(lambda: res[0, h, b], lambda: res[1, h, b], PRE)
        for kv in range(2):
            tm[h, kv, 2, b] = dkv[kv].astype(BF).reshape(4, 4, 64, HD)
        if hooks:
            hooks[2]()
            for rc in range(0, R, RC):
                rows = pl.ds(rc, RC)
                t = dot(Pm[rows, PRE:], res[0, h, b], NN)
                for i in range(PRE // KB):
                    t = t + dot(Pm[rows, pl.ds(i * KB, KB)], prefix_rows(h, 0, prompt, i), NN)
                dqacc[rows] = t
        @chunks
        def _(rc):
            rows = pl.ds(rc, RC)
            e = dqacc[rows] * INV
            if h == 0:
                dqh[b, rows] = e
            else:
                both = jnp.concatenate([dqh[b, rows].reshape(RC // G, G, HD), e.reshape(RC // G, G, HD)], axis=1)
                dqb[b, pl.ds(pl.multiple_of(rc // G, RC // G), RC // G)] = both.astype(BF)

    ends = []

    def swap_out(b, s, d):
        ends.append(mv.to(s.at[b, pl.ds(T2 * (1 - m), T2)], d.at[b, :, pl.ds(16 * m, 16)], mate))
        owns.append(mv.here(s.at[b, pl.ds(T2 * m, T2)], d.at[b, :, pl.ds(16 * m, 16)]))

    owns = []

    def trade(h, u):
        return mv.to(tm.at[h, 1 - c, 0:2, u], far.at[h, 0:2, u], sib)

    def pair_sum(h, u, cp):
        cp.wait_recv()

        @fours
        def _(k):
            for i in range(2):
                s0[h, i, u, k] = (tm[h, c, i, u, k].astype(F32) + far[h, i, u, k].astype(F32)).astype(BF)

        return ([mv.to(s0.at[h, 0, u, :, (x + 1 + d) % 4], r1.at[h, 0, d, u], xs[d]) for d in range(3)],
                [mv.to(s0.at[h, 1, u, (y + 1 + d) % 4], r1.at[h, 1, d, u], ys[d]) for d in range(3)])

    def second(h, cps):
        sent = []
        for a in range(2):
            for j in range(2):
                got(cps[j][a])

                @fours
                def _(k):
                    t = (s0[h, 0, j, k, x] if a == 0 else s0[h, 1, j, y, k]).astype(F32)
                    for d in range(3):
                        t = t + r1[h, a, d, j, k].astype(F32)
                    s1[h, a, j, k] = t.astype(BF)

            at = y if a == 0 else x
            for n in range(1, 8):
                sent.append(mv.to(s1.at[h, a, (zl + n // 4) % 2, (at + n % 4) % 4], r2.at[h, a, n - 1], (zy if a == 0 else zx)[n - 1]))
        return sent

    def final(h, cps):
        got(cps)
        for a in range(2):
            t = s1[h, a, zl, y if a == 0 else x].astype(F32)
            for n in range(7):
                t = t + r2[h, a, n].astype(F32)
            fin[c, h, a, x] = t.astype(BF)
        at = fin.at[c, h, :, x]
        ends.extend([mv.to(at, at, w) for w in xc])

    def trade_r(h, b):
        return mv.to(tm.at[h, 1 - c, 2, b], far.at[h, 2, b], sib)

    def pair_sum_r(h, b, cp):
        cp.wait_recv()

        @fours
        def _(k):
            s0[h, 2, b, k] = (tm[h, c, 2, b, k].astype(F32) + far[h, 2, b, k].astype(F32)).astype(BF)
        return [mv.to(s0.at[h, 2, b, (x + 1 + d) % 4], rr1.at[h, d, b], xs[d]) for d in range(3)]

    def final_r(h, b, cps):
        got(cps)

        @fours
        def _(k):
            t = s0[h, 2, b, x, k].astype(F32)
            for d in range(3):
                t = t + rr1[h, d, b, k].astype(F32)
            rs[h, b, k] = t.astype(BF)

        at = fr.at[c, 2 * m + h, b]
        owns.append(mv.here(rs.at[h, b, 2 * c + m], at))
        for core, part, w in ((1 - c, m, sib), (c, 1 - m, mate), (1 - c, 1 - m, cross)):
            ends.append(mv.to(rs.at[h, b, 2 * core + part], at, w))

    later = {}

    def resp_here():
        later["y"] = pass_z(pz, p1_at)
        vs.extend(pass_y(zl, vy, pv_at))
        got(rs0 + pass_r(0, rx0))

    pass_a(0, 0, resp_here)
    py2, ps = later["y"]
    vs += pass_y(1 - zl, vy2, pv_at)
    rs1 += pass_r(1, rx1)
    got(vs)
    pass_b(0, 0, lambda: got([g_in[0]]))
    ps += pass_y(zl, py, p1_at)
    got(rz1)
    rx2, rs2 = spread_r(2)
    pass_c(0, 0)
    t00 = trade_r(0, 0)
    ps += pass_y(1 - zl, py2, p1_at)
    got(ps + rs1)
    pass_a(1, 0)
    t00 = pair_sum_r(0, 0, t00)
    rs2 += pass_r(2, rx2)
    pass_b(1, 0)
    swap_out(0, ob, out)
    pass_c(1, 0)
    t10 = trade_r(1, 0)
    swap_out(0, dqb, dout)
    final_r(0, 0, t00)
    for cp in own_q[1]:
        cp.wait()
    got(q_in[1:] + g_in[1:] + rs2)
    pass_a(0, 1)
    t10 = pair_sum_r(1, 0, t10)
    pass_b(0, 1)
    pass_c(0, 1)
    a0 = [trade(0, 0), trade(0, 1)]
    t01 = trade_r(0, 1)
    final_r(1, 0, t10)
    pass_a(1, 1)
    a0 = [pair_sum(0, u, a0[u]) for u in range(2)]
    t01 = pair_sum_r(0, 1, t01)
    pass_b(1, 1)
    swap_out(1, ob, out)
    b0 = second(0, a0)
    t11, a1 = [None], [None, None]

    def after_first():
        a1[0] = trade(1, 0)
        final_r(0, 1, t01)

    def after_second():
        a1[1] = trade(1, 1)
        a1[0] = pair_sum(1, 0, a1[0])

    def after_resp():
        t11[0] = trade_r(1, 1)
        a1[1] = pair_sum(1, 1, a1[1])

    pass_c(1, 1, (after_first, after_second, after_resp))
    swap_out(1, dqb, dout)
    t11 = pair_sum_r(1, 1, t11[0])
    final(0, b0)
    b1 = second(1, a1)
    final_r(1, 1, t11)
    final(1, b1)
    got(ends)
    for cp in owns:
        cp.wait()
    mv.drain()


def fused(pid, plens, rlens, q, g, rk, rv, pk, pv):
    v = pltpu.VMEM
    n = 200
    return pl.pallas_call(
        kernel,
        out_shape=[jax.ShapeDtypeStruct((2, T2, 32, HD), BF)] * 2
        + [jax.ShapeDtypeStruct((2, 2, 2, 4, 64, HD), BF), jax.ShapeDtypeStruct((2, 4, 2, 64, HD), BF)],
        in_specs=[SM] * 3 + [HBM] * 2 + [VM] * 4,
        out_specs=[HBM, HBM, VM, VM],
        scratch_shapes=[
            v((2, T, 16, HD), BF), v((2, T, 16, HD), BF),
            v((2, 2, 1024, HD), BF), v((2, 2, 1024, HD), BF), v((2, 2, 2, 1024, HD), BF), v((2, 2, 2, 1024, HD), BF),
            v((R, PRE + RL), F32), v((R, PRE + RL), BF),
            v((R, 2 * HD), BF), v((R, HD), BF), v((R, HD), BF),
            v((R, 128), F32), v((R, 128), F32), v((R, HD), F32), v((R, HD), F32),
            v((2, 2, 2, 1024, HD), F32), v((2, R, HD), F32), v((2, R, HD), F32), v((2, T, 16, HD), BF), v((2, T, 16, HD), BF),
            v((2, 2, 3, 2, 4, 4, 64, HD), BF), v((2, 3, 2, 4, 4, 64, HD), BF), v((2, 3, 2, 4, 4, 64, HD), BF),
            v((2, 2, 3, 2, 4, 64, HD), BF), v((2, 2, 2, 4, 64, HD), BF),
            v((2, 2, 7, 64, HD), BF), v((2, 3, 2, 4, 64, HD), BF), v((2, 2, 4, 64, HD), BF),
            v((2, 4, 2, 64, HD), BF), v((2, 2, 2, 256, HD), BF),
            pltpu.SemaphoreType.DMA((n,)), pltpu.SemaphoreType.DMA((n,)), pltpu.SemaphoreType.DMA((32,)),
        ],
        compiler_params=pltpu.CompilerParams(collective_id=1, has_side_effects=True, vmem_limit_bytes=62 * 2**20),
    )(pid, plens, rlens, q, g, rk, rv, pk, pv)


def finish_kernel(out, dout, fin, fr, out2, dout2, dpk, dpv, drk, drv):
    out2[...] = out[...]
    dout2[...] = dout[...]
    for kv, (dp, dr) in enumerate(((dpk, drk), (dpv, drv))):
        for i in range(2):
            dp[i] = jnp.transpose(fin[kv, :, i], (1, 0, 2))
            dr[i] = jnp.transpose(fr[kv, :, i], (1, 0, 2))


def finish(out, dout, fin, fr):
    rows = jax.ShapeDtypeStruct((2, T2, 32, HD), BF)
    return pl.pallas_call(
        finish_kernel,
        out_shape=[rows] * 2 + [jax.ShapeDtypeStruct((2, 256, 2, HD), BF)] * 2 + [jax.ShapeDtypeStruct((2, T2, 4, HD), BF)] * 2,
        in_specs=[VM] * 4,
        out_specs=[VM] * 6,
        compiler_params=pltpu.CompilerParams(vmem_limit_bytes=60 * 2**20),
    )(out, dout, fin, fr)


def per_device(queries, resp_keys, resp_values, prefix_keys, prefix_values, grad_out, prompt_ids, prefix_lengths, resp_lengths):
    out, dout, fin, fr = fused(prompt_ids, prefix_lengths, resp_lengths, queries, grad_out, resp_keys, resp_values, prefix_keys, prefix_values)
    attention, d_queries, dpk, dpv, drk, drv = finish(out, dout, fin.reshape(2, 2, 2, 256, HD), fr)
    return (attention, d_queries, drk, drv, dpk, dpv)


def solution(mesh):
    rows = P("prefix", ("resp", "mp"), None, None)
    pre = P(None, "prefix", "mp", None)
    return jax.shard_map(
        per_device,
        mesh=mesh,
        in_specs=(rows, rows, rows, pre, pre, rows, P(), P(), P()),
        out_specs=(rows, rows, rows, rows, pre, pre),
        check_vma=False,
    )
```

```python
import math

import jax
import jax.numpy as jnp
from jax import lax
from jax.experimental import pallas as pl
from jax.experimental.pallas import tpu as pltpu
from jax.sharding import PartitionSpec as P

HD = 128
PRE = 2048
RL = 1024
T = 128
T2 = T // 2
G = 8
R = T * G
KB = 1024
RC = 256
NT = (((1,), (1,)), ((), ()))
NN = (((1,), (0,)), ((), ()))
TN = (((0,), (0,)), ((), ()))
MESH = pl.DeviceIdType.MESH
HBM = pl.BlockSpec(memory_space=pl.ANY)
VM = pl.BlockSpec(memory_space=pltpu.VMEM)
SM = pl.BlockSpec(memory_space=pltpu.SMEM)
BF = jnp.bfloat16
F32 = jnp.float32
INV = 1.0 / math.sqrt(HD)
C2 = math.log2(math.e) / math.sqrt(HD)


def dot(a, b, dims):
    return lax.dot_general(a, b, dims, preferred_element_type=F32)


class Mover:
    def __init__(self, send, recv, local):
        self.send, self.recv, self.local, self.n, self.m = send, recv, local, 0, 0
        self.remote = []

    def to(self, src, dst, where):
        cp = pltpu.make_async_remote_copy(
            src_ref=src, dst_ref=dst, send_sem=self.send.at[self.n], recv_sem=self.recv.at[self.n],
            device_id=where, device_id_type=MESH)
        self.n += 1
        cp.start()
        self.remote.append(cp)
        return cp

    def here(self, src, dst):
        cp = pltpu.make_async_copy(src, dst, self.local.at[self.m])
        self.m += 1
        cp.start()
        return cp

    def drain(self):
        for cp in self.remote:
            cp.wait_send()


def chunks(body):
    def step(n, _):
        body(pl.multiple_of(n * RC, RC))
        return 0

    lax.fori_loop(0, R // RC, step, 0)


def fours(body):
    def step(k, _):
        body(k)
        return 0

    lax.fori_loop(0, 4, step, 0)


def got(copies):
    for cp in copies:
        cp.wait_recv()


def kernel(pid, plen_ref, rlen_ref, q, g, rk_in, rv_in, pk_in, pv_in, out, dout, fin, fr,
           qb, gb, pk0, pv0, pre1, res, S, Pm, qhl, qr, dr, mx, ls, oacc, dqacc, X, oh, dqh, ob, dqb,
           tm, far, s0, r1, s1, r2, rr1, rs, rkt, pkt, send, recv, local):
    p, r, m = lax.axis_index("prefix"), lax.axis_index("resp"), lax.axis_index("mp")
    zl, y, x, c = p // 4, p % 4, r // 2, r % 2
    sib = {"resp": x * 2 + 1 - c}
    mate = {"mp": 1 - m}
    zmate = {"prefix": (1 - zl) * 4 + y}
    xs = [{"resp": ((x + d) % 4) * 2 + c} for d in (1, 2, 3)]
    ys = [{"prefix": zl * 4 + (y + d) % 4} for d in (1, 2, 3)]
    cross = {"resp": x * 2 + 1 - c, "mp": 1 - m}
    zy = [{"prefix": ((zl + dz) % 2) * 4 + (y + d) % 4} for dz in range(2) for d in range(4)][1:]
    zx = [{"prefix": ((zl + dz) % 2) * 4 + y, "resp": ((x + d) % 4) * 2 + c} for dz in range(2) for d in range(4)][1:]
    xc = [{"resp": ((x + d) % 4) * 2 + (c + dc) % 2} for dc in range(2) for d in range(4)][1:]
    mv = Mover(send, recv, local)
    pos0 = r * T
    mine_r = r * T
    half = c * 128

    own_q = [[mv.here(s.at[b, :, pl.ds(16 * m, 16)], d.at[b, pl.ds(T2 * m, T2)]) for s, d in ((q, qb), (g, gb))] for b in range(2)]
    for kv in range(2):
        for b in range(2):
            rkt[kv, :, b] = jnp.transpose((rk_in, rv_in)[kv][b], (1, 0, 2))
            pkt[kv, :, b] = jnp.transpose((pk_in, pv_in)[kv][b], (1, 0, 2))
    rk, rv, pk, pv = rkt.at[0], rkt.at[1], pkt.at[0], pkt.at[1]
    own_r = [mv.here(s.at[pl.ds(2 * m, 2)], res.at[kv, :, :, pl.ds(mine_r + m * T2, T2)]) for kv, s in enumerate((rk, rv))]
    own_p = [mv.here(pk.at[0], pk0.at[:, zl, pl.ds(y * 256, 256)]), mv.here(pv.at[0], pv0.at[:, zl, pl.ds(y * 256, 256)]),
             mv.here(pk.at[1], pre1.at[0, :, zl, pl.ds(y * 256, 256)]), mv.here(pv.at[1], pre1.at[1, :, zl, pl.ds(y * 256, 256)])]
    peers = [mate, cross] + zy + [zx[k] for k in (4, 5, 6)] + xc
    barrier = pltpu.get_barrier_semaphore()
    for peer in peers:
        pl.semaphore_signal(barrier, inc=1, device_id=peer, device_id_type=MESH)
    pl.semaphore_wait(barrier, len(peers))

    pk_at = lambda z, yy: pk0.at[:, z, pl.ds(yy * 256 + half, 128)]
    pv_at = lambda z, yy: pv0.at[:, z, pl.ds(yy * 256 + half, 128)]
    p1_at = lambda z, yy: pre1.at[:, :, z, pl.ds(yy * 256 + half, 128)]
    r_at = (lambda xx: res.at[:, 0, 0, pl.ds(xx * 256 + half, 128)], lambda xx: res.at[:, 1, 0, pl.ds(xx * 256 + half, 128)],
            lambda xx: res.at[:, :, 1, pl.ds(xx * 256 + half, 128)])

    def swap_in(b, s, d):
        return mv.to(s.at[b, :, pl.ds(16 * (1 - m), 16)], d.at[b, pl.ds(T2 * m, T2)], mate)

    def swap_r(b):
        return [mv.to(s.at[pl.ds(2 * (1 - m), 2), b], res.at[kv, :, b, pl.ds(mine_r + m * T2, T2)], mate) for kv, s in enumerate((rk, rv))]

    def spread_y(src, at):
        return [mv.to(src, at(zl, y), w) for w in ys]

    def pass_z(cp, at):
        got(cp if isinstance(cp, list) else [cp])
        return [mv.to(at(1 - zl, y), at(1 - zl, y), w) for w in ys], [mv.to(at(1 - zl, y), at(1 - zl, y), sib)]

    def pass_y(z, cps, at):
        sent = []
        for d in (0, 2, 1):
            yy = (y + 3 - d) % 4
            got(cps[d] if isinstance(cps[d], list) else [cps[d]])
            sent.append(mv.to(at(z, yy), at(z, yy), sib))
        return sent

    def spread_r(u):
        at = r_at[u](x)
        return [mv.to(at, at, w) for w in xs], [mv.to(at, at, sib)]

    def pass_r(u, cps):
        sent = []
        for d in (0, 2, 1):
            cps[d].wait_recv()
            at = r_at[u]((x + 3 - d) % 4)
            sent.append(mv.to(at, at, sib))
        return sent

    mine_k, mine_v = pk.at[0, :, pl.ds(half, 128)], pv.at[0, :, pl.ds(half, 128)]
    mine_1 = pk.at[1, :, pl.ds(half, 128)], pv.at[1, :, pl.ds(half, 128)]
    p1_of = lambda kv: pre1.at[kv, :, zl, pl.ds(y * 256 + half, 128)]
    kz = mv.to(mine_k, pk_at(zl, y), zmate)
    ky = spread_y(mine_k, pk_at)
    vz = mv.to(mine_v, pv_at(zl, y), zmate)
    rz0 = swap_r(0)
    q_in = [swap_in(0, q, qb), None]
    pz = [mv.to(mine_1[kv], p1_of(kv), zmate) for kv in range(2)]
    g_in = [swap_in(0, g, gb), None]
    rz1 = swap_r(1)
    q_in[1], g_in[1] = swap_in(1, q, qb), swap_in(1, g, gb)
    ky2, ks = pass_z(kz, pk_at)
    vy = spread_y(mine_v, pv_at)
    vy2, vs = pass_z(vz, pv_at)
    for cp in own_r:
        cp.wait()
    got(rz0)
    rx0, rs0 = spread_r(0)
    rx1, rs1 = spread_r(1)
    py = [[mv.to(mine_1[kv], p1_of(kv), w) for kv in range(2)] for w in ys]
    ks += pass_y(zl, ky, pk_at)
    ks += pass_y(1 - zl, ky2, pk_at)
    rs0 += pass_r(0, rx0)
    vs += pass_y(zl, vy, pv_at)
    for cp in own_q[0] + own_p:
        cp.wait()
    got([q_in[0]] + ks)

    def prefix_rows(h, kv, prompt, i):
        if h == 0:
            ref = pk0 if kv == 0 else pv0
            return ref[prompt, i]
        return pre1[kv, prompt, i]

    def limits(b, rc, resp):
        if not resp:
            return plen_ref[pid[2 * p + b]] - 1
        t = pos0 + rc // G + lax.broadcasted_iota(jnp.int32, (RC, 1), 0) // G
        return jnp.minimum(t, rlen_ref[2 * p + b] - 1)

    def head_rows(ref, b, h, rc):
        a = ref[b, pl.ds(pl.multiple_of(rc // G, RC // G), RC // G)].astype(F32)
        return a[:, h * G : (h + 1) * G].reshape(RC, HD)

    def pass_a(h, b, before_resp=None):
        prompt = pid[2 * p + b]
        @chunks
        def _(rc):
            rows = pl.ds(rc, RC)
            a = head_rows(qb, b, h, rc)
            qr[rows] = a.astype(BF)
            a = a * C2
            hi = a.astype(BF)
            qhl[rows, 0:HD] = hi
            qhl[rows, HD : 2 * HD] = (a - hi.astype(F32)).astype(BF)
        mx[...] = jnp.full_like(mx, -jnp.inf)

        def block(load, col0, base, resp):
            col = base + lax.broadcasted_iota(jnp.int32, (RC, KB), 1)

            kb = load()
            kk = jnp.concatenate([kb, kb], axis=1)
            for rc in range(0, R, RC):
                rows = pl.ds(rc, RC)
                s = dot(qhl[rows], kk, NT)
                s = jnp.where(col <= limits(b, rc, resp), s, -1e30)
                S[rows, pl.ds(col0, KB)] = s
                top = mx[rows]
                for k in range(0, KB, 128):
                    top = jnp.maximum(top, s[:, k : k + 128])
                mx[rows] = top

        def step(i, _):
            start = pl.multiple_of(i * KB, KB)
            block(lambda: prefix_rows(h, 0, prompt, i), start, start, False)
            return 0

        lax.fori_loop(0, PRE // KB, step, 0)
        if before_resp is not None:
            before_resp()
        block(lambda: res[0, h, b], PRE, 0, True)
        @chunks
        def _(rc):
            rows = pl.ds(rc, RC)
            mx[rows] = jnp.broadcast_to(jnp.max(mx[rows], axis=1, keepdims=True), (RC, 128))

    def pass_b(h, b, before_end=None):
        prompt = pid[2 * p + b]
        ls[...] = jnp.zeros_like(ls)
        oacc[...] = jnp.zeros_like(oacc)

        def block(load, col0):
            cols = pl.ds(col0, KB)

            vb = load()
            for rc in range(0, R, RC):
                rows = pl.ds(rc, RC)
                top = mx[rows]
                s = S[rows, cols]
                total = ls[rows]
                parts = []
                for k in range(0, KB, 128):
                    e = jnp.exp2(s[:, k : k + 128] - top)
                    total = total + e
                    parts.append(e.astype(BF))
                ls[rows] = total
                pb = jnp.concatenate(parts, axis=1)
                Pm[rows, cols] = pb
                oacc[rows] += dot(pb, vb, NN)

        def step(i, _):
            block(lambda: prefix_rows(h, 1, prompt, i), pl.multiple_of(i * KB, KB))
            return 0

        lax.fori_loop(0, PRE // KB, step, 0)
        block(lambda: res[1, h, b], PRE)
        if before_end is not None:
            before_end()
        @chunks
        def _(rc):
            rows = pl.ds(rc, RC)
            il = 1.0 / jnp.sum(ls[rows], axis=1, keepdims=True)
            o = (oacc[rows] * il).astype(BF).astype(F32)
            if h == 0:
                oh[b, rows] = o
            else:
                both = jnp.concatenate([oh[b, rows].reshape(RC // G, G, HD), o.reshape(RC // G, G, HD)], axis=1)
                ob[b, pl.ds(pl.multiple_of(rc // G, RC // G), RC // G)] = both.astype(BF)
            d = head_rows(gb, b, h, rc)
            t = pos0 + rc // G + lax.broadcasted_iota(jnp.int32, (RC, 1), 0) // G
            d = jnp.where(t < rlen_ref[2 * p + b], d, 0.0)
            delta = jnp.sum(d * o, axis=1, keepdims=True)
            dr[rows] = (d * il).astype(BF)
            mx[rows] = jnp.broadcast_to(delta * il, (RC, 128))

    def pass_c(h, b, hooks=()):
        prompt = pid[2 * p + b]
        if not hooks:
            dqacc[...] = jnp.zeros_like(dqacc)

        def block(load_k, load_v, col0):
            cols = pl.ds(col0, KB)
            dv = dot(dr[...], Pm[:, cols], TN).T

            vb, kb = load_v(), load_k()
            for rc in range(0, R, RC):
                rows = pl.ds(rc, RC)
                dp = dot(dr[rows], vb, NT)
                e = Pm[rows, cols].astype(F32)
                dl = mx[rows]
                ds = jnp.concatenate([e[:, k : k + 128] * (dp[:, k : k + 128] - dl) for k in range(0, KB, 128)], axis=1).astype(BF)
                Pm[rows, cols] = ds
                if not hooks:
                    dqacc[rows] += dot(ds, kb, NN)
            dk = dot(qr[...], Pm[:, cols], TN).T * INV
            return dk, dv

        def step(i, _):
            dkv = block(lambda: prefix_rows(h, 0, prompt, i), lambda: prefix_rows(h, 1, prompt, i), i * KB if isinstance(i, int) else pl.multiple_of(i * KB, KB))
            for kv in range(2):
                if b == 0:
                    X[h, kv, i] = dkv[kv]
                else:
                    before = pid[2 * p]
                    for a in range(2):
                        e = jnp.where(before == a, X[h, kv, i], 0.0) + jnp.where(prompt == a, dkv[kv], 0.0)
                        tm[h, kv, a, i] = e.astype(BF).reshape(4, 4, 64, HD)
            return 0

        if hooks:
            for i in range(PRE // KB):
                step(i, 0)
                hooks[i]()
        else:
            lax.fori_loop(0, PRE // KB, step, 0)
        dkv = block(lambda: res[0, h, b], lambda: res[1, h, b], PRE)
        for kv in range(2):
            tm[h, kv, 2, b] = dkv[kv].astype(BF).reshape(4, 4, 64, HD)
        if hooks:
            hooks[2]()
            for rc in range(0, R, RC):
                rows = pl.ds(rc, RC)
                t = dot(Pm[rows, PRE:], res[0, h, b], NN)
                for i in range(PRE // KB):
                    t = t + dot(Pm[rows, pl.ds(i * KB, KB)], prefix_rows(h, 0, prompt, i), NN)
                dqacc[rows] = t
            hooks[3]()
        @chunks
        def _(rc):
            rows = pl.ds(rc, RC)
            e = dqacc[rows] * INV
            if h == 0:
                dqh[b, rows] = e
            else:
                both = jnp.concatenate([dqh[b, rows].reshape(RC // G, G, HD), e.reshape(RC // G, G, HD)], axis=1)
                dqb[b, pl.ds(pl.multiple_of(rc // G, RC // G), RC // G)] = both.astype(BF)

    ends = []

    def swap_out(b, s, d):
        ends.append(mv.to(s.at[b, pl.ds(T2 * (1 - m), T2)], d.at[b, :, pl.ds(16 * m, 16)], mate))
        owns.append(mv.here(s.at[b, pl.ds(T2 * m, T2)], d.at[b, :, pl.ds(16 * m, 16)]))

    owns = []

    def trade(h, u):
        return mv.to(tm.at[h, 1 - c, 0:2, u], far.at[h, 0:2, u], sib)

    def pair_sum(h, u, cp):
        cp.wait_recv()

        @fours
        def _(k):
            for i in range(2):
                s0[h, i, u, k] = (tm[h, c, i, u, k].astype(F32) + far[h, i, u, k].astype(F32)).astype(BF)

        return ([mv.to(s0.at[h, 0, u, :, (x + 1 + d) % 4], r1.at[h, 0, d, u], xs[d]) for d in range(3)],
                [mv.to(s0.at[h, 1, u, (y + 1 + d) % 4], r1.at[h, 1, d, u], ys[d]) for d in range(3)])

    def second(h, cps):
        sent = []
        for a in range(2):
            for j in range(2):
                got(cps[j][a])

                @fours
                def _(k):
                    t = (s0[h, 0, j, k, x] if a == 0 else s0[h, 1, j, y, k]).astype(F32)
                    for d in range(3):
                        t = t + r1[h, a, d, j, k].astype(F32)
                    s1[h, a, j, k] = t.astype(BF)

            at = y if a == 0 else x
            for n in range(1, 8):
                sent.append(mv.to(s1.at[h, a, (zl + n // 4) % 2, (at + n % 4) % 4], r2.at[h, a, n - 1], (zy if a == 0 else zx)[n - 1]))
        return sent

    def final(h, cps):
        got(cps)
        for a in range(2):
            t = s1[h, a, zl, y if a == 0 else x].astype(F32)
            for n in range(7):
                t = t + r2[h, a, n].astype(F32)
            fin[c, h, a, x] = t.astype(BF)
        at = fin.at[c, h, :, x]
        ends.extend([mv.to(at, at, w) for w in xc])

    def trade_r(h, b):
        return mv.to(tm.at[h, 1 - c, 2, b], far.at[h, 2, b], sib)

    def pair_sum_r(h, b, cp):
        cp.wait_recv()

        @fours
        def _(k):
            s0[h, 2, b, k] = (tm[h, c, 2, b, k].astype(F32) + far[h, 2, b, k].astype(F32)).astype(BF)
        return [mv.to(s0.at[h, 2, b, (x + 1 + d) % 4], rr1.at[h, d, b], xs[d]) for d in range(3)]

    def final_r(h, b, cps):
        got(cps)

        @fours
        def _(k):
            t = s0[h, 2, b, x, k].astype(F32)
            for d in range(3):
                t = t + rr1[h, d, b, k].astype(F32)
            rs[h, b, k] = t.astype(BF)

        at = fr.at[c, 2 * m + h, b]
        owns.append(mv.here(rs.at[h, b, 2 * c + m], at))
        for core, part, w in ((1 - c, m, sib), (c, 1 - m, mate), (1 - c, 1 - m, cross)):
            ends.append(mv.to(rs.at[h, b, 2 * core + part], at, w))

    later = {}

    def resp_here():
        later["y"] = pass_z(pz, p1_at)
        vs.extend(pass_y(1 - zl, vy2, pv_at))
        got(rs0)

    pass_a(0, 0, resp_here)
    py2, ps = later["y"]
    rs1 += pass_r(1, rx1)
    got(vs)
    pass_b(0, 0, lambda: got([g_in[0]]))
    ps += pass_y(zl, py, p1_at)
    pass_c(0, 0)
    t00 = trade_r(0, 0)
    got(rz1)
    rx2, rs2 = spread_r(2)
    ps += pass_y(1 - zl, py2, p1_at)
    got(ps + rs1)
    pass_a(1, 0)
    t00 = pair_sum_r(0, 0, t00)
    rs2 += pass_r(2, rx2)
    pass_b(1, 0)
    swap_out(0, ob, out)
    pass_c(1, 0)
    t10 = trade_r(1, 0)
    swap_out(0, dqb, dout)
    final_r(0, 0, t00)
    for cp in own_q[1]:
        cp.wait()
    got(q_in[1:] + g_in[1:] + rs2)
    pass_a(0, 1)
    t10 = pair_sum_r(1, 0, t10)
    pass_b(0, 1)
    pass_c(0, 1)
    a0 = [trade(0, 0), trade(0, 1)]
    t01 = trade_r(0, 1)
    final_r(1, 0, t10)
    pass_a(1, 1)
    a0 = [pair_sum(0, u, a0[u]) for u in range(2)]
    t01 = pair_sum_r(0, 1, t01)
    pass_b(1, 1)
    swap_out(1, ob, out)
    t11, a1, b0 = [None], [None, None], []

    def after_first():
        a1[0] = trade(1, 0)
        b0.extend(second(0, a0))

    def after_second():
        a1[1] = trade(1, 1)
        a1[0] = pair_sum(1, 0, a1[0])
        final_r(0, 1, t01)

    def after_resp():
        t11[0] = trade_r(1, 1)

    def after_dq():
        a1[1] = pair_sum(1, 1, a1[1])

    pass_c(1, 1, (after_first, after_second, after_resp, after_dq))
    swap_out(1, dqb, dout)
    t11 = pair_sum_r(1, 1, t11[0])
    final(0, b0)
    b1 = second(1, a1)
    final_r(1, 1, t11)
    final(1, b1)
    got(ends)
    for cp in owns:
        cp.wait()
    mv.drain()


def fused(pid, plens, rlens, q, g, rk, rv, pk, pv):
    v = pltpu.VMEM
    n = 200
    return pl.pallas_call(
        kernel,
        out_shape=[jax.ShapeDtypeStruct((2, T2, 32, HD), BF)] * 2
        + [jax.ShapeDtypeStruct((2, 2, 2, 4, 64, HD), BF), jax.ShapeDtypeStruct((2, 4, 2, 64, HD), BF)],
        in_specs=[SM] * 3 + [HBM] * 2 + [VM] * 4,
        out_specs=[HBM, HBM, VM, VM],
        scratch_shapes=[
            v((2, T, 16, HD), BF), v((2, T, 16, HD), BF),
            v((2, 2, 1024, HD), BF), v((2, 2, 1024, HD), BF), v((2, 2, 2, 1024, HD), BF), v((2, 2, 2, 1024, HD), BF),
            v((R, PRE + RL), F32), v((R, PRE + RL), BF),
            v((R, 2 * HD), BF), v((R, HD), BF), v((R, HD), BF),
            v((R, 128), F32), v((R, 128), F32), v((R, HD), F32), v((R, HD), F32),
            v((2, 2, 2, 1024, HD), F32), v((2, R, HD), F32), v((2, R, HD), F32), v((2, T, 16, HD), BF), v((2, T, 16, HD), BF),
            v((2, 2, 3, 2, 4, 4, 64, HD), BF), v((2, 3, 2, 4, 4, 64, HD), BF), v((2, 3, 2, 4, 4, 64, HD), BF),
            v((2, 2, 3, 2, 4, 64, HD), BF), v((2, 2, 2, 4, 64, HD), BF),
            v((2, 2, 7, 64, HD), BF), v((2, 3, 2, 4, 64, HD), BF), v((2, 2, 4, 64, HD), BF),
            v((2, 4, 2, 64, HD), BF), v((2, 2, 2, 256, HD), BF),
            pltpu.SemaphoreType.DMA((n,)), pltpu.SemaphoreType.DMA((n,)), pltpu.SemaphoreType.DMA((32,)),
        ],
        compiler_params=pltpu.CompilerParams(collective_id=1, has_side_effects=True, vmem_limit_bytes=62 * 2**20),
    )(pid, plens, rlens, q, g, rk, rv, pk, pv)


def finish_kernel(out, dout, fin, fr, out2, dout2, dpk, dpv, drk, drv):
    out2[...] = out[...]
    dout2[...] = dout[...]
    for kv, (dp, dr) in enumerate(((dpk, drk), (dpv, drv))):
        for i in range(2):
            dp[i] = jnp.transpose(fin[kv, :, i], (1, 0, 2))
            dr[i] = jnp.transpose(fr[kv, :, i], (1, 0, 2))


def finish(out, dout, fin, fr):
    rows = jax.ShapeDtypeStruct((2, T2, 32, HD), BF)
    return pl.pallas_call(
        finish_kernel,
        out_shape=[rows] * 2 + [jax.ShapeDtypeStruct((2, 256, 2, HD), BF)] * 2 + [jax.ShapeDtypeStruct((2, T2, 4, HD), BF)] * 2,
        in_specs=[VM] * 4,
        out_specs=[VM] * 6,
        compiler_params=pltpu.CompilerParams(vmem_limit_bytes=60 * 2**20),
    )(out, dout, fin, fr)


def per_device(queries, resp_keys, resp_values, prefix_keys, prefix_values, grad_out, prompt_ids, prefix_lengths, resp_lengths):
    out, dout, fin, fr = fused(prompt_ids, prefix_lengths, resp_lengths, queries, grad_out, resp_keys, resp_values, prefix_keys, prefix_values)
    attention, d_queries, dpk, dpv, drk, drv = finish(out, dout, fin.reshape(2, 2, 2, 256, HD), fr)
    return (attention, d_queries, drk, drv, dpk, dpv)


def solution(mesh):
    rows = P("prefix", ("resp", "mp"), None, None)
    pre = P(None, "prefix", "mp", None)
    return jax.shard_map(
        per_device,
        mesh=mesh,
        in_specs=(rows, rows, rows, pre, pre, rows, P(), P(), P()),
        out_specs=(rows, rows, rows, rows, pre, pre),
        check_vma=False,
    )
```
